32 devices in a mesh: team: 4 (over x, core), row: 8 (over z, y).
Axes of the slice: x: 2, y: 2, z: 4, core: 2. Of those that a mesh axis runs over, the one named last changes fastest.
Arguments:
- features: bfloat16 [16384, 128], P(('team', 'row')), may hold values from -6 to 6
- tile_values: bfloat16 [128, 12, 256, 256], P(('team', 'row')), may hold values from 0 to 0.09375, as said below
- tile_row: int32 [128, 12], P(('team', 'row')), may hold values from 0 to 1
- tile_col: int32 [128, 12], P(('team', 'row')), may hold values from 0 to 15
- tile_count: int32 [128], P(('team', 'row')), may hold values from 1 to 12, as said below
- weight: bfloat16 [128, 256], replicated, may hold values from -0.5 to 0.5
- bias: float32 [256], replicated, may hold values from -1.5 to 1.5
- cotangent: bfloat16 [16384, 256], P(('team', 'row')), may hold values from -0.046875 to 0.046875
Outputs:
- hidden: bfloat16 [16384, 256], P(('team', 'row'))
- weight_grad: float32 [128, 256], replicated
- bias_grad: float32 [256], replicated
The draws below stay inside these ranges and needn't reach their ends.
Inputs may be any that keep to these rules, and one draw needn't show every extreme that they name: Live tiles stand in the first tile_count[g] slots of group g. In every draw some owner has 12 live tiles in each of its 4 groups. `tile_values`: every entry is a whole multiple of 1 / 32; most entries are zero.
All inputs are finite; a program needn't handle non-finite values.
Results may differ from the reference program's by a relative error of at most 0.0052.
Values may be sent and summed in bfloat16 or wider, within the bound.
A program may use at most 128 MiB of HBM per device.

```python
import jax
import jax.numpy as jnp
from jax import lax

FIN = 128
FOUT = 256
BLK = 256
ROW_BLOCKS = 2
SLOTS = 12
NODES = 16384
N_TEAM = 4
N_ROW = 8
DEVICES = 32


def draw_tile_values(key, part):
    key = jax.random.fold_in(key, 5)
    key_mask, key_level = jax.random.split(key, 2)
    shape = (DEVICES * N_TEAM, SLOTS, BLK, BLK)
    present = jax.random.randint(key_mask, shape, 0, 64) == 0
    levels = jax.random.randint(key_level, shape, 1, 4)
    return (jnp.where(present, levels, 0).astype(jnp.float32) * (1.0 / 32.0)).astype(jnp.bfloat16)


def draw_tile_count(key, part):
    key = jax.random.fold_in(key, 11)
    key_base, key_hot, key_forced = jax.random.split(key, 3)
    base = jax.random.randint(key_base, (DEVICES * N_TEAM,), 1, SLOTS // 2 + 1)
    hot_draw = jax.random.randint(key_hot, (DEVICES,), 0, 16) == 0
    forced = jax.random.randint(key_forced, (), 0, DEVICES)
    hot_owner = hot_draw | (jnp.arange(DEVICES) == forced)
    hot_group = jnp.repeat(hot_owner, N_TEAM)
    return jnp.where(hot_group, SLOTS, base).astype(jnp.int32)


def plant(array, key, least, largest):
    dims = array.shape
    spot = [jax.random.randint(jax.random.fold_in(key, axis), (), 0, dims[axis]) for axis in range(len(dims))]
    array = array.at[tuple(spot)].set(least)
    longest = dims.index(max(dims))
    spot[longest] = (spot[longest] + 1) % dims[longest]
    return array.at[tuple(spot)].set(largest)


def steps_of(rng, dims, pieces, smallest, top_value):
    gain, own = 1.0, jax.random.fold_in(rng, 6)
    for position, parts in pieces:
        heights = jnp.exp(jax.random.uniform(jax.random.fold_in(own, position), (parts,), jnp.float32, smallest / len(pieces), top_value / len(pieces)))
        gain = gain * jnp.repeat(heights, dims[position] // parts).reshape([-1 if axis == position else 1 for axis in range(len(dims))])
    return gain


def scatter_about(rng, shape, spread, reach, shards=(), kind=jnp.bfloat16):
    drawn = jax.random.normal(rng, shape, jnp.float32) * spread
    if len(shards) > 0:
        drawn = steps_of(rng, shape, shards, -0.22, 0.18) * drawn
    return jnp.clip(drawn, min=-reach, max=reach).astype(kind)


def setup_inputs(seed: int = 0) -> dict:
    keys = jax.random.split(jax.random.key(seed), 9)
    features = scatter_about(keys[0], (NODES, FIN), 1.0, 6.0, ((0, 32),))
    tile_values = draw_tile_values(jax.random.fold_in(keys[8], 71), 0)
    tile_row = plant(jax.random.randint(keys[2], (DEVICES * N_TEAM, SLOTS), 0, ROW_BLOCKS), jax.random.fold_in(keys[2], 1), 0, ROW_BLOCKS - 1).astype(jnp.int32)
    tile_col = plant(jax.random.randint(keys[3], (DEVICES * N_TEAM, SLOTS), 0, N_ROW * ROW_BLOCKS), jax.random.fold_in(keys[3], 1), 0, (N_ROW * ROW_BLOCKS) - 1).astype(jnp.int32)
    tile_count = draw_tile_count(jax.random.fold_in(keys[8], 71), 0)
    weight = scatter_about(keys[5], (FIN, FOUT), FIN ** -0.5, 0.5)
    bias = scatter_about(keys[6], (FOUT,), 0.25, 1.5, (), jnp.float32)
    cotangent = scatter_about(keys[7], (NODES, FOUT), NODES ** -0.5, 0.046875, ((0, 32),))
    return {"features": features, "tile_values": tile_values, "tile_row": tile_row, "tile_col": tile_col, "tile_count": tile_count, "weight": weight, "bias": bias, "cotangent": cotangent}


def gelu_parts(values):
    gelu_coef = 0.7978845608
    tangent_h = jnp.tanh(gelu_coef * (values + 0.044715 * values * values * values))
    result = 0.5 * values * (1.0 + tangent_h)
    derive = 0.5 * (1.0 + tangent_h) + 0.5 * values * (1.0 - tangent_h * tangent_h) * gelu_coef * (1.0 + 3.0 * 0.044715 * values * values)
    return result, derive


def reference(features, tile_values, tile_row, tile_col, tile_count, weight, bias, cotangent):
    groups = tile_count.shape[0]
    owners = groups // N_TEAM
    block_feats = features.reshape(-1, BLK, FIN).astype(jnp.float32)
    panel_blocks = N_ROW * ROW_BLOCKS
    slot_ids = jnp.arange(SLOTS, dtype=jnp.int32)
    block_ids = jnp.arange(ROW_BLOCKS, dtype=jnp.int32)

    def add_group(total, group_id):
        owner = (group_id // N_TEAM).astype(jnp.int32)
        column_team = (group_id % N_TEAM).astype(jnp.int32)
        tiles = lax.dynamic_index_in_dim(tile_values, group_id, 0, False).astype(jnp.float32)
        col_index = column_team * panel_blocks + lax.dynamic_index_in_dim(tile_col, group_id, 0, False)
        row_index = lax.dynamic_index_in_dim(tile_row, group_id, 0, False)
        count = lax.dynamic_index_in_dim(tile_count, group_id, 0, False)
        picked = jnp.take(block_feats, col_index.astype(jnp.int32), axis=0)
        products = jnp.einsum("sij,sjf->sif", tiles, picked, precision=lax.Precision.HIGHEST)
        live_mask = slot_ids < count
        row_select = ((row_index[None, :] == block_ids[:, None]) & live_mask[None, :]).astype(jnp.float32)
        summed = jnp.einsum("rs,sif->rif", row_select, products, precision=lax.Precision.HIGHEST)
        start = (owner * ROW_BLOCKS).astype(jnp.int32)
        current = lax.dynamic_slice_in_dim(total, start, ROW_BLOCKS, 0)
        total = lax.dynamic_update_slice_in_dim(total, current + summed, start, 0)
        return total, None

    empty = jnp.zeros((owners * ROW_BLOCKS, BLK, FIN), jnp.float32)
    total, unused = lax.scan(add_group, empty, jnp.arange(groups, dtype=jnp.int32))
    aggregated = total.reshape(-1, FIN).astype(jnp.bfloat16)
    pre = jnp.dot(aggregated, weight, preferred_element_type=jnp.float32) + bias
    result, derive = gelu_parts(pre)
    hidden = result.astype(jnp.bfloat16)
    slope = cotangent.astype(jnp.float32) * derive
    slope_half = slope.astype(jnp.bfloat16)
    weight_grad = lax.dot_general(aggregated, slope_half, (((0,), (0,)), ((), ())), preferred_element_type=jnp.float32)
    bias_grad = jnp.sum(slope, axis=0)
    return hidden, weight_grad, bias_grad
```

```python
import functools

import jax
import jax.numpy as jnp
from jax import lax
from jax.experimental import pallas as pl
from jax.experimental.pallas import tpu as pltpu
from jax.sharding import PartitionSpec as P

MESH = pl.DeviceIdType.MESH
GROUP = 16
LANES = 128


def gelu_parts(values):
    gelu_coef = 0.7978845608
    tangent_h = jnp.tanh(gelu_coef * (values + 0.044715 * values * values * values))
    result = 0.5 * values * (1.0 + tangent_h)
    derive = 0.5 * (1.0 + tangent_h) + 0.5 * values * (1.0 - tangent_h * tangent_h) * gelu_coef * (
        1.0 + 3.0 * 0.044715 * values * values
    )
    return (result, derive)


def flip(value, bits):
    result = value
    weight = 1
    while weight <= bits:
        if bits & weight:
            bit = lax.rem(lax.div(value, weight), 2)
            result = result + weight * (1 - 2 * bit)
        weight *= 2
    return result


def kernel(
    n_row,
    features,
    tile_values,
    tile_row,
    tile_col,
    tile_count,
    weight,
    bias,
    cotangent,
    hidden_out,
    weight_out,
    bias_out,
    near,
    near_other,
    far,
    far_other,
    tiles,
    weight_v,
    bias_v,
    cot_v,
    hidden_v,
    total,
    part,
    pair,
    red,
    scattered,
    bias_in,
    owned,
    crossed,
    fin,
    fin_other,
    local_sem,
    tile_sem,
    z_sem,
    x_sem,
    y_sem,
    xd_sem,
    yd_sem,
    core_sem,
    pair_sem,
    rs_sem,
    rb_sem,
    cross_sem,
    ag_sem,
    ab_sem,
):
    team, row = lax.axis_index("team"), lax.axis_index("row")
    a, core = lax.div(team, 2), lax.rem(team, 2)
    z, b = lax.div(row, 2), lax.rem(row, 2)
    n_z = n_row // 2
    slots = tile_values.shape[1]
    blk = tile_values.shape[2]

    x_dev = ((1 - a) * 2 + core, row)
    y_dev = (team, z * 2 + (1 - b))
    c_dev = (a * 2 + (1 - core), row)

    def rows_of(z_now, b_now):
        return pl.ds(2 * (z_now * 2 + b_now), 2)

    own = rows_of(z, b)
    load_own = pltpu.make_async_copy(features, near.at[own], local_sem.at[0])
    load_own.start()
    panels = [a * 2 + core, a * 2 + 1 - core, (1 - a) * 2 + core, (1 - a) * 2 + 1 - core]
    loads = [
        pltpu.make_async_copy(weight, weight_v, local_sem.at[1]),
        pltpu.make_async_copy(bias, bias_v, local_sem.at[2]),
        pltpu.make_async_copy(cotangent, cot_v, local_sem.at[3]),
    ]
    tile_loads = [
        pltpu.make_async_copy(tile_values.at[panel], tiles.at[i], tile_sem.at[i])
        for i, panel in enumerate(panels)
    ]

    barrier = pltpu.get_barrier_semaphore()
    greeted = [c_dev]
    for i in range(1, 2 * n_row):
        flat = lax.rem(a * n_row + row + i, 2 * n_row)
        greeted.append((lax.div(flat, n_row) * 2 + core, lax.rem(flat, n_row)))
    for dev in greeted:
        pl.semaphore_signal(barrier, inc=1, device_id=dev, device_id_type=MESH)
    for copy in tile_loads + loads:
        copy.start()
    pl.semaphore_wait(barrier, len(greeted))
    load_own.wait()

    sent = []

    def remote(src, dst, sems, i, dev):
        return pltpu.make_async_remote_copy(
            src_ref=src,
            dst_ref=dst,
            send_sem=sems.at[0, i],
            recv_sem=sems.at[1, i],
            device_id=dev,
            device_id_type=MESH,
        )

    def send(src, dst, sems, i, dev):
        copy = remote(src, dst, sems, i, dev)
        copy.start()
        sent.append(copy)

    def arrived(ref, sems, i, dev):
        remote(ref, ref, sems, i, dev).wait_recv()

    def full(j):
        z_now = flip(z, j)
        rows = rows_of(z_now, b)
        if j > 0:
            arrived(near.at[rows], z_sem, j, (team, z_now * 2 + b))
        send(near.at[rows], near.at[rows], y_sem, j, y_dev)
        send(near.at[rows], far.at[rows], x_sem, j, x_dev)
        if j == 0:
            for k in range(1, n_z):
                dev = (team, flip(z, k) * 2 + b)
                send(near.at[rows], near.at[rows], z_sem, k, dev)
        send(near.at[rows], near_other.at[rows], core_sem, j, c_dev)

    def diagonal(j):
        z_now = flip(z, j)
        mine, other = rows_of(z_now, b), rows_of(z_now, 1 - b)
        arrived(near.at[other], y_sem, j, y_dev)
        second = 2 * (z_now * 2 + 1 - b) + 1
        send(near.at[second], far.at[second], xd_sem, j, x_dev)
        send(near.at[other], near_other.at[other], core_sem, n_z + j, c_dev)
        arrived(far.at[mine], x_sem, j, x_dev)
        first = 2 * (z_now * 2 + b)
        send(far.at[first], far.at[first], yd_sem, j, y_dev)
        send(far.at[mine], far_other.at[mine], core_sem, 2 * n_z + j, c_dev)

    def last(j):
        other = rows_of(flip(z, j), 1 - b)
        first = 2 * (flip(z, j) * 2 + 1 - b)
        arrived(far.at[first + 1], xd_sem, j, x_dev)
        arrived(far.at[first], yd_sem, j, y_dev)
        send(far.at[other], far_other.at[other], core_sem, 3 * n_z + j, c_dev)

    def from_core(ref, first, b_now):
        for j in range(n_z):
            rows = rows_of(flip(z, j), b_now)
            arrived(ref.at[rows], core_sem, first * n_z + j, c_dev)

    def aggregate(i, feats):
        tile_loads[i].wait()
        panel = panels[i]
        count = tile_count[panel]
        step = 6 if slots % 6 == 0 else slots
        for base in range(0, slots, step):
            left, right = [], []
            for s in range(base, base + step):
                block = feats[tile_col[panel, s]]
                live = s < count
                place = tile_row[panel, s]
                zero = jnp.zeros_like(block)
                upper = jnp.where(live & (place == 0), block, zero)
                lower = jnp.where(live & (place == 1), block, zero)
                left.append(tiles[i, s])
                right.append(jnp.concatenate([upper, lower], axis=1))
            product = jnp.dot(
                jnp.concatenate(left, axis=1),
                jnp.concatenate(right, axis=0),
                preferred_element_type=jnp.float32,
            )
            if i == 0 and base == 0:
                total[...] = product
            else:
                total[...] += product

    full(0)
    for j in range(1, n_z):
        full(j)
        diagonal(j - 1)
    diagonal(n_z - 1)
    aggregate(0, near)
    for j in range(n_z // 2):
        last(j)
    from_core(near_other, 0, b)
    from_core(near_other, 1, 1 - b)
    aggregate(1, near_other)
    for j in range(n_z // 2, n_z):
        last(j)
    aggregate(2, far)
    from_core(far_other, 2, b)
    from_core(far_other, 3, 1 - b)
    aggregate(3, far_other)

    for copy in loads:
        copy.wait()
    step = 128
    weight_part = jnp.zeros((weight_v.shape[0], weight_v.shape[1]), jnp.float32)
    bias_part = jnp.zeros((1, weight_v.shape[1]), jnp.float32)
    for r in range(0, 2 * blk, step):
        lane = (r // blk) * LANES
        inner = r % blk
        agg = total[inner : inner + step, lane : lane + LANES].astype(jnp.bfloat16)
        pre = jnp.dot(agg, weight_v[...], preferred_element_type=jnp.float32) + bias_v[...]
        result, derive = gelu_parts(pre)
        hidden_v[r : r + step, :] = result.astype(jnp.bfloat16)
        slope = cot_v[r : r + step, :].astype(jnp.float32) * derive
        weight_part = weight_part + lax.dot_general(
            agg,
            slope.astype(jnp.bfloat16),
            (((0,), (0,)), ((), ())),
            preferred_element_type=jnp.float32,
        )
        bias_part = bias_part + jnp.sum(slope, axis=0, keepdims=True)
    for h in range(2):
        lanes = slice(h * LANES, (h + 1) * LANES)
        part[h, 0:GROUP] = weight_part[:, lanes].reshape(GROUP, 8, LANES)
        part[h, GROUP] = jnp.broadcast_to(bias_part[:, lanes], (8, LANES))
    store_hidden = pltpu.make_async_copy(hidden_v, hidden_out, local_sem.at[0])
    store_hidden.start()

    send(part.at[1 - core], pair, pair_sem, 0, c_dev)
    arrived(pair, pair_sem, 0, c_dev)
    red[...] = part[core] + pair[...]

    group, member = lax.div(row, 8), a * 8 + lax.rem(row, 8)

    def at(member_now, group_now):
        return (lax.div(member_now, 8) * 2 + core, group_now * 8 + lax.rem(member_now, 8))

    head = at(0, group)
    for i in range(1, GROUP):
        peer = lax.rem(member + i, GROUP)
        send(red.at[peer], scattered.at[member], rs_sem, i, at(peer, group))

    @pl.when(member != 0)
    def _():
        copy = pltpu.make_async_remote_copy(
            src_ref=red.at[GROUP],
            dst_ref=bias_in.at[member],
            send_sem=rb_sem.at[0, 0],
            recv_sem=rb_sem.at[1, member],
            device_id=head,
            device_id_type=MESH,
        )
        copy.start()
        copy.wait_send()

    scattered[member] = red[member]
    owned[1] = jnp.zeros((8, LANES), jnp.float32)
    for i in range(1, GROUP):
        peer = lax.rem(member + GROUP - i, GROUP)
        arrived(scattered.at[peer], rs_sem, i, at(peer, group))
    owned[0] = jnp.sum(scattered[...], axis=0)

    @pl.when(member == 0)
    def _():
        bias_in[0] = red[GROUP]
        for i in range(1, GROUP):
            remote(bias_in.at[i], bias_in.at[i], rb_sem, i, c_dev).wait_recv()
        owned[1] = jnp.sum(bias_in[...], axis=0)

    n_group = n_row // 8
    if n_group > 1:
        for g in range(1, n_group):
            dev = at(member, lax.rem(group + g, n_group))
            send(owned, crossed.at[g], cross_sem, g, dev)
        crossed[0] = owned[...]
        for g in range(1, n_group):
            arrived(crossed.at[g], cross_sem, g, at(member, lax.rem(group + n_group - g, n_group)))
        for g in range(1, n_group):
            sent.pop().wait_send()
        ordered = jnp.zeros(owned.shape, jnp.float32)
        for g in range(n_group):
            ordered = ordered + crossed[lax.rem(group + n_group - g, n_group)]
        owned[...] = ordered

    for i in range(1, GROUP):
        peer = lax.rem(member + i, GROUP)
        send(owned.at[0], fin.at[member], ag_sem, i, at(peer, group))

    @pl.when(member == 0)
    def _():
        copies = [
            remote(owned.at[1], fin.at[GROUP], ab_sem, i, at(i, group)) for i in range(1, GROUP)
        ]
        for copy in copies:
            copy.start()
        fin[GROUP] = owned[1]
        for copy in copies:
            copy.wait_send()

    @pl.when(member != 0)
    def _():
        pltpu.make_async_remote_copy(
            src_ref=owned.at[1],
            dst_ref=fin.at[GROUP],
            send_sem=ab_sem.at[0, 0],
            recv_sem=ab_sem.at[1, member],
            device_id=head,
            device_id_type=MESH,
        ).wait_recv()

    fin[member] = owned[0]
    for i in range(1, GROUP):
        peer = lax.rem(member + GROUP - i, GROUP)
        arrived(fin.at[peer], ag_sem, i, at(peer, group))
    send(fin, fin_other, pair_sem, 1, c_dev)
    arrived(fin_other, pair_sem, 1, c_dev)
    mine, other = fin[...], fin_other[...]
    for h in range(2):
        half = jnp.where(core == h, mine, other)
        lanes = slice(h * LANES, (h + 1) * LANES)
        weight_out[:, lanes] = half[0:GROUP].reshape(GROUP * 8, LANES)
        bias_out[:, lanes] = half[GROUP, 0:1]
    for copy in sent:
        copy.wait_send()
    store_hidden.wait()


def local(n_row, features, tile_values, tile_row, tile_col, tile_count, weight, bias, cotangent):
    n_panel, slots, blk, _ = tile_values.shape
    rows, width = features.shape
    wide = weight.shape[1]
    n_z = n_row // 2
    n_group = n_row // 8
    dma = pltpu.SemaphoreType.DMA
    anywhere = pl.BlockSpec(memory_space=pl.ANY)
    smem = pl.BlockSpec(memory_space=pltpu.SMEM)
    vmem = pl.BlockSpec(memory_space=pltpu.VMEM)
    hidden, weight_grad, bias_grad = pl.pallas_call(
        functools.partial(kernel, n_row),
        out_shape=[
            jax.ShapeDtypeStruct((rows, wide), jnp.bfloat16),
            jax.ShapeDtypeStruct((width, wide), jnp.float32),
            jax.ShapeDtypeStruct((1, wide), jnp.float32),
        ],
        in_specs=[anywhere, anywhere, smem, smem, smem, anywhere, anywhere, anywhere],
        out_specs=[anywhere, vmem, vmem],
        scratch_shapes=[
            pltpu.VMEM((2 * n_row, blk, width), jnp.bfloat16),
            pltpu.VMEM((2 * n_row, blk, width), jnp.bfloat16),
            pltpu.VMEM((2 * n_row, blk, width), jnp.bfloat16),
            pltpu.VMEM((2 * n_row, blk, width), jnp.bfloat16),
            pltpu.VMEM((n_panel, slots, blk, blk), jnp.bfloat16),
            pltpu.VMEM((width, wide), jnp.bfloat16),
            pltpu.VMEM((1, wide), jnp.float32),
            pltpu.VMEM((rows, wide), jnp.bfloat16),
            pltpu.VMEM((rows, wide), jnp.bfloat16),
            pltpu.VMEM((blk, 2 * width), jnp.float32),
            pltpu.VMEM((2, GROUP + 1, 8, LANES), jnp.float32),
            pltpu.VMEM((GROUP + 1, 8, LANES), jnp.float32),
            pltpu.VMEM((GROUP + 1, 8, LANES), jnp.float32),
            pltpu.VMEM((GROUP, 8, LANES), jnp.float32),
            pltpu.VMEM((GROUP, 8, LANES), jnp.float32),
            pltpu.VMEM((2, 8, LANES), jnp.float32),
            pltpu.VMEM((n_group, 2, 8, LANES), jnp.float32),
            pltpu.VMEM((GROUP + 1, 8, LANES), jnp.float32),
            pltpu.VMEM((GROUP + 1, 8, LANES), jnp.float32),
            dma((4,)),
            dma((4,)),
            dma((2, n_z)),
            dma((2, n_z)),
            dma((2, n_z)),
            dma((2, n_z)),
            dma((2, n_z)),
            dma((2, 4 * n_z)),
            dma((2, 2)),
            dma((2, GROUP)),
            dma((2, GROUP)),
            dma((2, n_group)),
            dma((2, GROUP)),
            dma((2, GROUP)),
        ],
        compiler_params=pltpu.CompilerParams(
            collective_id=0, has_side_effects=True, vmem_limit_bytes=56 * 1024 * 1024
        ),
    )(
        features.reshape(rows // blk, blk, width),
        tile_values,
        tile_row,
        tile_col,
        tile_count,
        weight,
        bias.reshape(1, wide),
        cotangent,
    )
    return (hidden, weight_grad, bias_grad.reshape(wide))


def solution(mesh):
    in_specs = (
        P(("team", "row"), None),
        P(("team", "row"), None, None, None),
        P(("team", "row"), None),
        P(("team", "row"), None),
        P(("team", "row")),
        P(),
        P(),
        P(("team", "row"), None),
    )
    out_specs = (P(("team", "row"), None), P(), P())
    return jax.shard_map(
        functools.partial(local, mesh.shape["row"]),
        mesh=mesh,
        in_specs=in_specs,
        out_specs=out_specs,
        check_vma=False,
    )
```

```python
import functools

import jax
import jax.numpy as jnp
from jax import lax
from jax.experimental import pallas as pl
from jax.experimental.pallas import tpu as pltpu
from jax.sharding import PartitionSpec as P

MESH = pl.DeviceIdType.MESH
GROUP = 16
LANES = 128


def gelu_parts(values):
    gelu_coef = 0.7978845608
    tangent_h = jnp.tanh(gelu_coef * (values + 0.044715 * values * values * values))
    result = 0.5 * values * (1.0 + tangent_h)
    derive = 0.5 * (1.0 + tangent_h) + 0.5 * values * (1.0 - tangent_h * tangent_h) * gelu_coef * (
        1.0 + 3.0 * 0.044715 * values * values
    )
    return (result, derive)


def flip(value, bits):
    result = value
    weight = 1
    while weight <= bits:
        if bits & weight:
            bit = lax.rem(lax.div(value, weight), 2)
            result = result + weight * (1 - 2 * bit)
        weight *= 2
    return result


def kernel(
    n_row,
    features,
    tile_values,
    tile_row,
    tile_col,
    tile_count,
    weight,
    bias,
    cotangent,
    hidden_out,
    weight_out,
    bias_out,
    near,
    near_other,
    far,
    far_other,
    tiles,
    weight_v,
    bias_v,
    cot_v,
    hidden_v,
    total,
    part,
    pair,
    red,
    scattered,
    bias_in,
    owned,
    crossed,
    fin,
    fin_other,
    wg,
    bg,
    local_sem,
    tile_sem,
    z_sem,
    x_sem,
    y_sem,
    xd_sem,
    yd_sem,
    core_sem,
    pair_sem,
    rs_sem,
    rb_sem,
    cross_sem,
    ag_sem,
    ab_sem,
):
    team, row = lax.axis_index("team"), lax.axis_index("row")
    a, core = lax.div(team, 2), lax.rem(team, 2)
    z, b = lax.div(row, 2), lax.rem(row, 2)
    n_z = n_row // 2
    slots = tile_values.shape[1]
    blk = tile_values.shape[2]

    x_dev = ((1 - a) * 2 + core, row)
    y_dev = (team, z * 2 + (1 - b))
    c_dev = (a * 2 + (1 - core), row)

    def rows_of(z_now, b_now):
        return pl.ds(2 * (z_now * 2 + b_now), 2)

    own = rows_of(z, b)
    load_own = pltpu.make_async_copy(features, near.at[own], local_sem.at[0])
    load_own.start()
    panels = [a * 2 + core, a * 2 + 1 - core, (1 - a) * 2 + core, (1 - a) * 2 + 1 - core]
    loads = [
        pltpu.make_async_copy(weight, weight_v, local_sem.at[1]),
        pltpu.make_async_copy(bias, bias_v, local_sem.at[2]),
        pltpu.make_async_copy(cotangent, cot_v, local_sem.at[3]),
    ]
    tile_loads = [
        pltpu.make_async_copy(tile_values.at[panel], tiles.at[i], tile_sem.at[i])
        for i, panel in enumerate(panels)
    ]

    barrier = pltpu.get_barrier_semaphore()
    greeted = [c_dev]
    for i in range(1, 2 * n_row):
        flat = lax.rem(a * n_row + row + i, 2 * n_row)
        greeted.append((lax.div(flat, n_row) * 2 + core, lax.rem(flat, n_row)))
    for dev in greeted:
        pl.semaphore_signal(barrier, inc=1, device_id=dev, device_id_type=MESH)
    for copy in tile_loads + loads:
        copy.start()
    pl.semaphore_wait(barrier, len(greeted))
    load_own.wait()

    sent = []

    def remote(src, dst, sems, i, dev):
        return pltpu.make_async_remote_copy(
            src_ref=src,
            dst_ref=dst,
            send_sem=sems.at[0, i],
            recv_sem=sems.at[1, i],
            device_id=dev,
            device_id_type=MESH,
        )

    def send(src, dst, sems, i, dev):
        copy = remote(src, dst, sems, i, dev)
        copy.start()
        return copy

    def arrived(ref, sems, i, dev):
        remote(ref, ref, sems, i, dev).wait_recv()

    def full(source):
        rows = rows_of(source, b)
        send(near.at[rows], near.at[rows], y_sem, source, y_dev)
        send(near.at[rows], far.at[rows], x_sem, source, x_dev)
        send(near.at[rows], near_other.at[rows], core_sem, source, c_dev)

    def pass_on(source, way):
        rows = rows_of(source, b)
        dev = (team, (z + 1 - 2 * way) * 2 + b)

        def copy():
            return remote(near.at[rows], near.at[rows], z_sem, way * n_z + source, dev)

        @pl.when(z < n_z - 1 if way == 0 else z > 0)
        def _():
            copy().start()

    def diagonal(source):
        mine, other = rows_of(source, b), rows_of(source, 1 - b)
        arrived(near.at[other], y_sem, source, y_dev)
        second = 2 * (source * 2 + 1 - b) + 1
        send(near.at[second], far.at[second], xd_sem, source, x_dev)
        send(near.at[other], near_other.at[other], core_sem, n_z + source, c_dev)
        arrived(far.at[mine], x_sem, source, x_dev)
        first = 2 * (source * 2 + b)
        send(far.at[first], far.at[first], yd_sem, source, y_dev)
        send(far.at[mine], far_other.at[mine], core_sem, 2 * n_z + source, c_dev)

    def last(source):
        other = rows_of(source, 1 - b)
        first = 2 * (source * 2 + 1 - b)
        arrived(far.at[first + 1], xd_sem, source, x_dev)
        arrived(far.at[first], yd_sem, source, y_dev)
        send(far.at[other], far_other.at[other], core_sem, 3 * n_z + source, c_dev)

    def both_ways(t, act):
        for way in range(2):
            source = z - t if way == 0 else z + t

            @pl.when(source >= 0 if way == 0 else source < n_z)
            def _():
                act(source, way)

    def receive(source, way):
        rows = rows_of(source, b)
        dev = (team, (z - 1 + 2 * way) * 2 + b)
        arrived(near.at[rows], z_sem, way * n_z + source, dev)
        pass_on(source, way)
        full(source)

    def from_core(ref, first, b_now):
        for j in range(n_z):
            arrived(ref.at[rows_of(j, b_now)], core_sem, first * n_z + j, c_dev)

    def all_sent():
        for way in range(2):
            for source in range(n_z):
                goes = (z < n_z - 1) & (z >= source) if way == 0 else (z > 0) & (z <= source)
                rows = rows_of(source, b)

                @pl.when(goes)
                def _():
                    remote(near.at[rows], near.at[rows], z_sem, way * n_z + source, c_dev).wait_send()

        for source in range(n_z):
            rows = rows_of(source, b)
            for sems in (y_sem, x_sem):
                remote(near.at[rows], near.at[rows], sems, source, c_dev).wait_send()
            for sems in (xd_sem, yd_sem):
                one = near.at[2 * source]
                remote(one, one, sems, source, c_dev).wait_send()
            for kind in range(4):
                remote(near.at[rows], near.at[rows], core_sem, kind * n_z + source, c_dev).wait_send()

    def aggregate(i, feats):
        tile_loads[i].wait()
        panel = panels[i]
        count = tile_count[panel]
        step = 4 if slots % 4 == 0 else slots

        def add(base, carry):
            left, right = [], []
            for k in range(step):
                s = base * step + k
                block = feats[tile_col[panel, s]]
                live = s < count
                place = tile_row[panel, s]
                zero = jnp.zeros_like(block)
                upper = jnp.where(live & (place == 0), block, zero)
                lower = jnp.where(live & (place == 1), block, zero)
                left.append(tiles[i, s])
                right.append(jnp.concatenate([upper, lower], axis=1))
            total[...] += jnp.dot(
                jnp.concatenate(left, axis=1),
                jnp.concatenate(right, axis=0),
                preferred_element_type=jnp.float32,
            )
            return carry

        lax.fori_loop(0, slots // step, add, 0)

    pass_on(z, 0)
    pass_on(z, 1)
    full(z)
    total[...] = jnp.zeros_like(total)
    wg[...] = jnp.zeros_like(wg)
    bg[...] = jnp.zeros_like(bg)
    for t in range(1, n_z):
        both_ways(t, receive)
        if t == 1:
            diagonal(z)
        else:
            both_ways(t - 1, lambda source, way: diagonal(source))
    both_ways(n_z - 1, lambda source, way: diagonal(source))
    aggregate(0, near)
    last(z)
    for t in range(1, n_z // 2):
        both_ways(t, lambda source, way: last(source))
    from_core(near_other, 0, b)
    from_core(near_other, 1, 1 - b)
    aggregate(1, near_other)
    for t in range(n_z // 2, n_z):
        both_ways(t, lambda source, way: last(source))
    aggregate(2, far)
    from_core(far_other, 2, b)
    from_core(far_other, 3, 1 - b)
    aggregate(3, far_other)

    for copy in loads:
        copy.wait()
    step = 128
    for h in range(2):

        def layer(k, carry):
            inner = pl.ds(pl.multiple_of(k * step, step), step)
            outer = pl.ds(pl.multiple_of(h * blk + k * step, step), step)
            agg = total[inner, h * LANES : (h + 1) * LANES].astype(jnp.bfloat16)
            pre = jnp.dot(agg, weight_v[...], preferred_element_type=jnp.float32) + bias_v[...]
            result, derive = gelu_parts(pre)
            hidden_v[outer, :] = result.astype(jnp.bfloat16)
            slope = cot_v[outer, :].astype(jnp.float32) * derive
            wg[...] += lax.dot_general(
                agg,
                slope.astype(jnp.bfloat16),
                (((0,), (0,)), ((), ())),
                preferred_element_type=jnp.float32,
            )
            bg[...] += jnp.sum(slope, axis=0, keepdims=True)
            return carry

        lax.fori_loop(0, blk // step, layer, 0)
    weight_part, bias_part = wg[...], bg[...]
    for h in range(2):
        lanes = slice(h * LANES, (h + 1) * LANES)
        part[h, 0:GROUP] = weight_part[:, lanes].reshape(GROUP, 8, LANES)
        part[h, GROUP] = jnp.broadcast_to(bias_part[:, lanes], (8, LANES))
    store_hidden = pltpu.make_async_copy(hidden_v, hidden_out, local_sem.at[0])
    store_hidden.start()

    sent.append(send(part.at[1 - core], pair, pair_sem, 0, c_dev))
    arrived(pair, pair_sem, 0, c_dev)
    red[...] = part[core] + pair[...]

    group, member = lax.div(row, 8), a * 8 + lax.rem(row, 8)

    def at(member_now, group_now):
        return (lax.div(member_now, 8) * 2 + core, group_now * 8 + lax.rem(member_now, 8))

    head = at(0, group)
    for i in range(1, GROUP):
        peer = lax.rem(member + i, GROUP)
        sent.append(send(red.at[peer], scattered.at[member], rs_sem, i, at(peer, group)))

    @pl.when(member != 0)
    def _():
        copy = pltpu.make_async_remote_copy(
            src_ref=red.at[GROUP],
            dst_ref=bias_in.at[member],
            send_sem=rb_sem.at[0, 0],
            recv_sem=rb_sem.at[1, member],
            device_id=head,
            device_id_type=MESH,
        )
        copy.start()
        copy.wait_send()

    scattered[member] = red[member]
    owned[1] = jnp.zeros((8, LANES), jnp.float32)
    for i in range(1, GROUP):
        peer = lax.rem(member + GROUP - i, GROUP)
        arrived(scattered.at[peer], rs_sem, i, at(peer, group))
    owned[0] = jnp.sum(scattered[...], axis=0)

    @pl.when(member == 0)
    def _():
        bias_in[0] = red[GROUP]
        for i in range(1, GROUP):
            remote(bias_in.at[i], bias_in.at[i], rb_sem, i, c_dev).wait_recv()
        owned[1] = jnp.sum(bias_in[...], axis=0)

    n_group = n_row // 8
    if n_group > 1:
        for g in range(1, n_group):
            dev = at(member, lax.rem(group + g, n_group))
            sent.append(send(owned, crossed.at[g], cross_sem, g, dev))
        crossed[0] = owned[...]
        for g in range(1, n_group):
            arrived(crossed.at[g], cross_sem, g, at(member, lax.rem(group + n_group - g, n_group)))
        for g in range(1, n_group):
            sent.pop().wait_send()
        ordered = jnp.zeros(owned.shape, jnp.float32)
        for g in range(n_group):
            ordered = ordered + crossed[lax.rem(group + n_group - g, n_group)]
        owned[...] = ordered

    for i in range(1, GROUP):
        peer = lax.rem(member + i, GROUP)
        sent.append(send(owned.at[0], fin.at[member], ag_sem, i, at(peer, group)))

    @pl.when(member == 0)
    def _():
        copies = [
            remote(owned.at[1], fin.at[GROUP], ab_sem, i, at(i, group)) for i in range(1, GROUP)
        ]
        for copy in copies:
            copy.start()
        fin[GROUP] = owned[1]
        for copy in copies:
            copy.wait_send()

    @pl.when(member != 0)
    def _():
        pltpu.make_async_remote_copy(
            src_ref=owned.at[1],
            dst_ref=fin.at[GROUP],
            send_sem=ab_sem.at[0, 0],
            recv_sem=ab_sem.at[1, member],
            device_id=head,
            device_id_type=MESH,
        ).wait_recv()

    fin[member] = owned[0]
    for i in range(1, GROUP):
        peer = lax.rem(member + GROUP - i, GROUP)
        arrived(fin.at[peer], ag_sem, i, at(peer, group))
    sent.append(send(fin, fin_other, pair_sem, 1, c_dev))
    arrived(fin_other, pair_sem, 1, c_dev)
    mine, other = fin[...], fin_other[...]
    for h in range(2):
        half = jnp.where(core == h, mine, other)
        lanes = slice(h * LANES, (h + 1) * LANES)
        weight_out[:, lanes] = half[0:GROUP].reshape(GROUP * 8, LANES)
        bias_out[:, lanes] = half[GROUP, 0:1]
    for copy in sent:
        copy.wait_send()
    all_sent()
    store_hidden.wait()


def hand_over(hidden, weight_grad, bias_grad, hidden_out, weight_out, bias_out, sems):
    copies = [
        pltpu.make_async_copy(hidden, hidden_out, sems.at[0]),
        pltpu.make_async_copy(weight_grad, weight_out, sems.at[1]),
        pltpu.make_async_copy(bias_grad, bias_out, sems.at[2]),
    ]
    for copy in copies:
        copy.start()
    for copy in copies:
        copy.wait()


def local(n_row, features, tile_values, tile_row, tile_col, tile_count, weight, bias, cotangent):
    n_panel, slots, blk, _ = tile_values.shape
    rows, width = features.shape
    wide = weight.shape[1]
    n_z = n_row // 2
    n_group = n_row // 8
    dma = pltpu.SemaphoreType.DMA
    anywhere = pl.BlockSpec(memory_space=pl.ANY)
    smem = pl.BlockSpec(memory_space=pltpu.SMEM)
    vmem = pl.BlockSpec(memory_space=pltpu.VMEM)
    hidden, weight_grad, bias_grad = pl.pallas_call(
        functools.partial(kernel, n_row),
        out_shape=[
            jax.ShapeDtypeStruct((rows, wide), jnp.bfloat16),
            jax.ShapeDtypeStruct((width, wide), jnp.float32),
            jax.ShapeDtypeStruct((1, wide), jnp.float32),
        ],
        in_specs=[anywhere, anywhere, smem, smem, smem, anywhere, anywhere, anywhere],
        out_specs=[anywhere, vmem, vmem],
        scratch_shapes=[
            pltpu.VMEM((2 * n_row, blk, width), jnp.bfloat16),
            pltpu.VMEM((2 * n_row, blk, width), jnp.bfloat16),
            pltpu.VMEM((2 * n_row, blk, width), jnp.bfloat16),
            pltpu.VMEM((2 * n_row, blk, width), jnp.bfloat16),
            pltpu.VMEM((n_panel, slots, blk, blk), jnp.bfloat16),
            pltpu.VMEM((width, wide), jnp.bfloat16),
            pltpu.VMEM((1, wide), jnp.float32),
            pltpu.VMEM((rows, wide), jnp.bfloat16),
            pltpu.VMEM((rows, wide), jnp.bfloat16),
            pltpu.VMEM((blk, 2 * width), jnp.float32),
            pltpu.VMEM((2, GROUP + 1, 8, LANES), jnp.float32),
            pltpu.VMEM((GROUP + 1, 8, LANES), jnp.float32),
            pltpu.VMEM((GROUP + 1, 8, LANES), jnp.float32),
            pltpu.VMEM((GROUP, 8, LANES), jnp.float32),
            pltpu.VMEM((GROUP, 8, LANES), jnp.float32),
            pltpu.VMEM((2, 8, LANES), jnp.float32),
            pltpu.VMEM((n_group, 2, 8, LANES), jnp.float32),
            pltpu.VMEM((GROUP + 1, 8, LANES), jnp.float32),
            pltpu.VMEM((GROUP + 1, 8, LANES), jnp.float32),
            pltpu.VMEM((width, wide), jnp.float32),
            pltpu.VMEM((1, wide), jnp.float32),
            dma((4,)),
            dma((4,)),
            dma((2, 2 * n_z)),
            dma((2, n_z)),
            dma((2, n_z)),
            dma((2, n_z)),
            dma((2, n_z)),
            dma((2, 4 * n_z)),
            dma((2, 2)),
            dma((2, GROUP)),
            dma((2, GROUP)),
            dma((2, n_group)),
            dma((2, GROUP)),
            dma((2, GROUP)),
        ],
        compiler_params=pltpu.CompilerParams(
            collective_id=0, has_side_effects=True, vmem_limit_bytes=56 * 1024 * 1024
        ),
    )(
        features.reshape(rows // blk, blk, width),
        tile_values,
        tile_row,
        tile_col,
        tile_count,
        weight,
        bias.reshape(1, wide),
        cotangent,
    )
    shapes = [jax.ShapeDtypeStruct(x.shape, x.dtype) for x in (hidden, weight_grad, bias_grad)]
    hidden, weight_grad, bias_grad = pl.pallas_call(
        hand_over,
        out_shape=shapes,
        in_specs=[anywhere] * 3,
        out_specs=[anywhere] * 3,
        scratch_shapes=[dma((3,))],
        compiler_params=pltpu.CompilerParams(vmem_limit_bytes=60 * 1024 * 1024),
    )(hidden, weight_grad, bias_grad)
    return (hidden, weight_grad, bias_grad.reshape(wide))


def solution(mesh):
    in_specs = (
        P(("team", "row"), None),
        P(("team", "row"), None, None, None),
        P(("team", "row"), None),
        P(("team", "row"), None),
        P(("team", "row")),
        P(),
        P(),
        P(("team", "row"), None),
    )
    out_specs = (P(("team", "row"), None), P(), P())
    return jax.shard_map(
        functools.partial(local, mesh.shape["row"]),
        mesh=mesh,
        in_specs=in_specs,
        out_specs=out_specs,
        check_vma=False,
    )
```

```python
import functools

import jax
import jax.numpy as jnp
from jax import lax
from jax.experimental import pallas as pl
from jax.experimental.pallas import tpu as pltpu
from jax.sharding import PartitionSpec as P

MESH = pl.DeviceIdType.MESH
GROUP = 16
LANES = 128


def gelu_parts(values):
    gelu_coef = 0.7978845608
    tangent_h = jnp.tanh(gelu_coef * (values + 0.044715 * values * values * values))
    result = 0.5 * values * (1.0 + tangent_h)
    derive = 0.5 * (1.0 + tangent_h) + 0.5 * values * (1.0 - tangent_h * tangent_h) * gelu_coef * (
        1.0 + 3.0 * 0.044715 * values * values
    )
    return (result, derive)


def flip(value, bits):
    result = value
    weight = 1
    while weight <= bits:
        if bits & weight:
            bit = lax.rem(lax.div(value, weight), 2)
            result = result + weight * (1 - 2 * bit)
        weight *= 2
    return result


def kernel(
    n_row,
    features,
    tile_values,
    tile_row,
    tile_col,
    tile_count,
    weight,
    bias,
    cotangent,
    hidden_out,
    weight_out,
    bias_out,
    near,
    near_other,
    far,
    far_other,
    tiles,
    weight_v,
    bias_v,
    cot_v,
    hidden_v,
    total,
    part,
    pair,
    red,
    scattered,
    bias_in,
    owned,
    crossed,
    fin,
    fin_other,
    wg,
    bg,
    local_sem,
    tile_sem,
    z_sem,
    x_sem,
    y_sem,
    xd_sem,
    yd_sem,
    zd_sem,
    core_sem,
    pair_sem,
    rs_sem,
    rb_sem,
    cross_sem,
    ag_sem,
    ab_sem,
):
    team, row = lax.axis_index("team"), lax.axis_index("row")
    a, core = lax.div(team, 2), lax.rem(team, 2)
    z, b = lax.div(row, 2), lax.rem(row, 2)
    n_z = n_row // 2
    slots = tile_values.shape[1]
    blk = tile_values.shape[2]

    x_dev = ((1 - a) * 2 + core, row)
    y_dev = (team, z * 2 + (1 - b))
    c_dev = (a * 2 + (1 - core), row)

    def rows_of(z_now, b_now):
        return pl.ds(2 * (z_now * 2 + b_now), 2)

    own = rows_of(z, b)
    load_own = pltpu.make_async_copy(features, near.at[own], local_sem.at[0])
    load_own.start()
    panels = [a * 2 + core, a * 2 + 1 - core, (1 - a) * 2 + core, (1 - a) * 2 + 1 - core]
    loads = [
        pltpu.make_async_copy(weight, weight_v, local_sem.at[1]),
        pltpu.make_async_copy(bias, bias_v, local_sem.at[2]),
        pltpu.make_async_copy(cotangent, cot_v, local_sem.at[3]),
    ]
    tile_loads = [
        pltpu.make_async_copy(tile_values.at[panel], tiles.at[i], tile_sem.at[i])
        for i, panel in enumerate(panels)
    ]

    barrier = pltpu.get_barrier_semaphore()
    greeted = [c_dev]
    for i in range(1, 2 * n_row):
        flat = lax.rem(a * n_row + row + i, 2 * n_row)
        greeted.append((lax.div(flat, n_row) * 2 + core, lax.rem(flat, n_row)))
    for dev in greeted:
        pl.semaphore_signal(barrier, inc=1, device_id=dev, device_id_type=MESH)
    for copy in tile_loads + loads:
        copy.start()
    pl.semaphore_wait(barrier, len(greeted))
    load_own.wait()

    sent = []

    def remote(src, dst, sems, i, dev):
        return pltpu.make_async_remote_copy(
            src_ref=src,
            dst_ref=dst,
            send_sem=sems.at[0, i],
            recv_sem=sems.at[1, i],
            device_id=dev,
            device_id_type=MESH,
        )

    def send(src, dst, sems, i, dev):
        copy = remote(src, dst, sems, i, dev)
        copy.start()
        return copy

    def arrived(ref, sems, i, dev):
        remote(ref, ref, sems, i, dev).wait_recv()

    def full(source):
        rows = rows_of(source, b)
        send(near.at[rows], near.at[rows], y_sem, source, y_dev)
        send(near.at[rows], far.at[rows], x_sem, source, x_dev)
        send(near.at[rows], near_other.at[rows], core_sem, source, c_dev)

    def pass_on(source, way):
        rows = rows_of(source, b)
        dev = (team, (z + 1 - 2 * way) * 2 + b)

        def copy():
            return remote(near.at[rows], near.at[rows], z_sem, way * n_z + source, dev)

        @pl.when(z < n_z - 1 if way == 0 else z > 0)
        def _():
            copy().start()

    def diagonal(source, crosses):
        mine, other = rows_of(source, b), rows_of(source, 1 - b)
        arrived(near.at[other], y_sem, source, y_dev)
        if crosses:
            second = 2 * (source * 2 + 1 - b) + 1
            send(near.at[second], far.at[second], xd_sem, source, x_dev)
        send(near.at[other], near_other.at[other], core_sem, n_z + source, c_dev)
        arrived(far.at[mine], x_sem, source, x_dev)
        if crosses:
            first = 2 * (source * 2 + b)
            send(far.at[first], far.at[first], yd_sem, source, y_dev)
        send(far.at[mine], far_other.at[mine], core_sem, 2 * n_z + source, c_dev)

    z_pair = (team, flip(z, 1) * 2 + b)

    def last(source, crosses):
        other = rows_of(source, 1 - b)
        first = 2 * (source * 2 + 1 - b)
        if crosses:
            arrived(far.at[first + 1], xd_sem, source, x_dev)
            arrived(far.at[first], yd_sem, source, y_dev)
            send(far.at[other], far.at[other], zd_sem, source, z_pair)
        else:
            arrived(far.at[other], zd_sem, source, z_pair)
        send(far.at[other], far_other.at[other], core_sem, 3 * n_z + source, c_dev)

    def both_ways(t, act):
        for way in range(2):
            source = z - t if way == 0 else z + t

            @pl.when(source >= 0 if way == 0 else source < n_z)
            def _():
                act(source, way)

    def receive(source, way):
        rows = rows_of(source, b)
        dev = (team, (z - 1 + 2 * way) * 2 + b)
        arrived(near.at[rows], z_sem, way * n_z + source, dev)
        pass_on(source, way)
        full(source)

    def from_core(ref, first, b_now):
        for j in range(n_z):
            arrived(ref.at[rows_of(j, b_now)], core_sem, first * n_z + j, c_dev)

    def all_sent():
        for way in range(2):
            for source in range(n_z):
                goes = (z < n_z - 1) & (z >= source) if way == 0 else (z > 0) & (z <= source)
                rows = rows_of(source, b)

                @pl.when(goes)
                def _():
                    remote(near.at[rows], near.at[rows], z_sem, way * n_z + source, c_dev).wait_send()

        for source in range(n_z):
            rows = rows_of(source, b)
            for sems in (y_sem, x_sem):
                remote(near.at[rows], near.at[rows], sems, source, c_dev).wait_send()

            @pl.when(lax.rem(z, 2) == source % 2)
            def _():
                one = near.at[2 * source]
                for sems in (xd_sem, yd_sem):
                    remote(one, one, sems, source, c_dev).wait_send()
                remote(near.at[rows], near.at[rows], zd_sem, source, c_dev).wait_send()

            for kind in range(4):
                remote(near.at[rows], near.at[rows], core_sem, kind * n_z + source, c_dev).wait_send()

    def aggregate(i, feats):
        tile_loads[i].wait()
        panel = panels[i]
        count = tile_count[panel]
        step = 4 if slots % 4 == 0 else slots

        def add(base, carry):
            left, right = [], []
            for k in range(step):
                s = base * step + k
                block = feats[tile_col[panel, s]]
                live = s < count
                place = tile_row[panel, s]
                zero = jnp.zeros_like(block)
                upper = jnp.where(live & (place == 0), block, zero)
                lower = jnp.where(live & (place == 1), block, zero)
                left.append(tiles[i, s])
                right.append(jnp.concatenate([upper, lower], axis=1))
            total[...] += jnp.dot(
                jnp.concatenate(left, axis=1),
                jnp.concatenate(right, axis=0),
                preferred_element_type=jnp.float32,
            )
            return carry

        lax.fori_loop(0, slots // step, add, 0)

    pass_on(z, 0)
    pass_on(z, 1)
    full(z)
    total[...] = jnp.zeros_like(total)
    wg[...] = jnp.zeros_like(wg)
    bg[...] = jnp.zeros_like(bg)
    def step_of(act, t):
        if t == 0:
            act(z, True)
        else:
            both_ways(t, lambda source, way: act(source, t % 2 == 0))

    for t in range(1, n_z):
        both_ways(t, receive)
        if t == 1:
            step_of(diagonal, 0)
        if t % 2 == 0:
            step_of(diagonal, t - 1)
            step_of(last, t - 2)
            step_of(diagonal, t)
    step_of(last, n_z - 2)
    step_of(diagonal, n_z - 1)
    step_of(last, 1)
    aggregate(0, near)
    for t in range(3, n_z, 2):
        step_of(last, t)
    from_core(near_other, 0, b)
    from_core(near_other, 1, 1 - b)
    aggregate(1, near_other)
    aggregate(2, far)
    from_core(far_other, 2, b)
    from_core(far_other, 3, 1 - b)
    aggregate(3, far_other)

    for copy in loads:
        copy.wait()
    step = 128
    for h in range(2):

        def layer(k, carry):
            inner = pl.ds(pl.multiple_of(k * step, step), step)
            outer = pl.ds(pl.multiple_of(h * blk + k * step, step), step)
            agg = total[inner, h * LANES : (h + 1) * LANES].astype(jnp.bfloat16)
            pre = jnp.dot(agg, weight_v[...], preferred_element_type=jnp.float32) + bias_v[...]
            result, derive = gelu_parts(pre)
            hidden_v[outer, :] = result.astype(jnp.bfloat16)
            slope = cot_v[outer, :].astype(jnp.float32) * derive
            wg[...] += lax.dot_general(
                agg,
                slope.astype(jnp.bfloat16),
                (((0,), (0,)), ((), ())),
                preferred_element_type=jnp.float32,
            )
            bg[...] += jnp.sum(slope, axis=0, keepdims=True)
            return carry

        lax.fori_loop(0, blk // step, layer, 0)
    weight_part, bias_part = wg[...], bg[...]
    for h in range(2):
        lanes = slice(h * LANES, (h + 1) * LANES)
        part[h, 0:GROUP] = weight_part[:, lanes].reshape(GROUP, 8, LANES)
        part[h, GROUP] = jnp.broadcast_to(bias_part[:, lanes], (8, LANES))
    store_hidden = pltpu.make_async_copy(hidden_v, hidden_out, local_sem.at[0])
    store_hidden.start()

    sent.append(send(part.at[1 - core], pair, pair_sem, 0, c_dev))
    arrived(pair, pair_sem, 0, c_dev)
    red[...] = part[core] + pair[...]

    group, member = lax.div(row, 8), a * 8 + lax.rem(row, 8)

    def at(member_now, group_now):
        return (lax.div(member_now, 8) * 2 + core, group_now * 8 + lax.rem(member_now, 8))

    head = at(0, group)
    for i in range(1, GROUP):
        peer = lax.rem(member + i, GROUP)
        sent.append(send(red.at[peer], scattered.at[member], rs_sem, i, at(peer, group)))

    @pl.when(member != 0)
    def _():
        copy = pltpu.make_async_remote_copy(
            src_ref=red.at[GROUP],
            dst_ref=bias_in.at[member],
            send_sem=rb_sem.at[0, 0],
            recv_sem=rb_sem.at[1, member],
            device_id=head,
            device_id_type=MESH,
        )
        copy.start()
        copy.wait_send()

    scattered[member] = red[member]
    owned[1] = jnp.zeros((8, LANES), jnp.float32)
    for i in range(1, GROUP):
        peer = lax.rem(member + GROUP - i, GROUP)
        arrived(scattered.at[peer], rs_sem, i, at(peer, group))
    owned[0] = jnp.sum(scattered[...], axis=0)

    @pl.when(member == 0)
    def _():
        bias_in[0] = red[GROUP]
        for i in range(1, GROUP):
            remote(bias_in.at[i], bias_in.at[i], rb_sem, i, c_dev).wait_recv()
        owned[1] = jnp.sum(bias_in[...], axis=0)

    n_group = n_row // 8
    if n_group > 1:
        for g in range(1, n_group):
            dev = at(member, lax.rem(group + g, n_group))
            sent.append(send(owned, crossed.at[g], cross_sem, g, dev))
        crossed[0] = owned[...]
        for g in range(1, n_group):
            arrived(crossed.at[g], cross_sem, g, at(member, lax.rem(group + n_group - g, n_group)))
        for g in range(1, n_group):
            sent.pop().wait_send()
        ordered = jnp.zeros(owned.shape, jnp.float32)
        for g in range(n_group):
            ordered = ordered + crossed[lax.rem(group + n_group - g, n_group)]
        owned[...] = ordered

    for i in range(1, GROUP):
        peer = lax.rem(member + i, GROUP)
        sent.append(send(owned.at[0], fin.at[member], ag_sem, i, at(peer, group)))

    @pl.when(member == 0)
    def _():
        copies = [
            remote(owned.at[1], fin.at[GROUP], ab_sem, i, at(i, group)) for i in range(1, GROUP)
        ]
        for copy in copies:
            copy.start()
        fin[GROUP] = owned[1]
        for copy in copies:
            copy.wait_send()

    @pl.when(member != 0)
    def _():
        pltpu.make_async_remote_copy(
            src_ref=owned.at[1],
            dst_ref=fin.at[GROUP],
            send_sem=ab_sem.at[0, 0],
            recv_sem=ab_sem.at[1, member],
            device_id=head,
            device_id_type=MESH,
        ).wait_recv()

    fin[member] = owned[0]
    for i in range(1, GROUP):
        peer = lax.rem(member + GROUP - i, GROUP)
        arrived(fin.at[peer], ag_sem, i, at(peer, group))
    sent.append(send(fin, fin_other, pair_sem, 1, c_dev))
    arrived(fin_other, pair_sem, 1, c_dev)
    mine, other = fin[...], fin_other[...]
    for h in range(2):
        half = jnp.where(core == h, mine, other)
        lanes = slice(h * LANES, (h + 1) * LANES)
        weight_out[:, lanes] = half[0:GROUP].reshape(GROUP * 8, LANES)
        bias_out[:, lanes] = half[GROUP, 0:1]
    for copy in sent:
        copy.wait_send()
    all_sent()
    store_hidden.wait()


def hand_over(*refs):
    ins, outs, held, load_sem, store_sem = refs[0:3], refs[3:6], refs[6:9], refs[9], refs[10]
    loads = [pltpu.make_async_copy(ins[i], held[i], load_sem.at[i]) for i in range(3)]
    stores = [pltpu.make_async_copy(held[i], outs[i], store_sem.at[i]) for i in range(3)]
    for copy in loads:
        copy.start()
    for load, store in zip(loads, stores):
        load.wait()
        store.start()
    for copy in stores:
        copy.wait()


def local(n_row, features, tile_values, tile_row, tile_col, tile_count, weight, bias, cotangent):
    n_panel, slots, blk, _ = tile_values.shape
    rows, width = features.shape
    wide = weight.shape[1]
    n_z = n_row // 2
    n_group = n_row // 8
    dma = pltpu.SemaphoreType.DMA
    anywhere = pl.BlockSpec(memory_space=pl.ANY)
    smem = pl.BlockSpec(memory_space=pltpu.SMEM)
    vmem = pl.BlockSpec(memory_space=pltpu.VMEM)
    hidden, weight_grad, bias_grad = pl.pallas_call(
        functools.partial(kernel, n_row),
        out_shape=[
            jax.ShapeDtypeStruct((rows, wide), jnp.bfloat16),
            jax.ShapeDtypeStruct((width, wide), jnp.float32),
            jax.ShapeDtypeStruct((1, wide), jnp.float32),
        ],
        in_specs=[anywhere, anywhere, smem, smem, smem, anywhere, anywhere, anywhere],
        out_specs=[anywhere, vmem, vmem],
        scratch_shapes=[
            pltpu.VMEM((2 * n_row, blk, width), jnp.bfloat16),
            pltpu.VMEM((2 * n_row, blk, width), jnp.bfloat16),
            pltpu.VMEM((2 * n_row, blk, width), jnp.bfloat16),
            pltpu.VMEM((2 * n_row, blk, width), jnp.bfloat16),
            pltpu.VMEM((n_panel, slots, blk, blk), jnp.bfloat16),
            pltpu.VMEM((width, wide), jnp.bfloat16),
            pltpu.VMEM((1, wide), jnp.float32),
            pltpu.VMEM((rows, wide), jnp.bfloat16),
            pltpu.VMEM((rows, wide), jnp.bfloat16),
            pltpu.VMEM((blk, 2 * width), jnp.float32),
            pltpu.VMEM((2, GROUP + 1, 8, LANES), jnp.float32),
            pltpu.VMEM((GROUP + 1, 8, LANES), jnp.float32),
            pltpu.VMEM((GROUP + 1, 8, LANES), jnp.float32),
            pltpu.VMEM((GROUP, 8, LANES), jnp.float32),
            pltpu.VMEM((GROUP, 8, LANES), jnp.float32),
            pltpu.VMEM((2, 8, LANES), jnp.float32),
            pltpu.VMEM((n_group, 2, 8, LANES), jnp.float32),
            pltpu.VMEM((GROUP + 1, 8, LANES), jnp.float32),
            pltpu.VMEM((GROUP + 1, 8, LANES), jnp.float32),
            pltpu.VMEM((width, wide), jnp.float32),
            pltpu.VMEM((1, wide), jnp.float32),
            dma((4,)),
            dma((4,)),
            dma((2, 2 * n_z)),
            dma((2, n_z)),
            dma((2, n_z)),
            dma((2, n_z)),
            dma((2, n_z)),
            dma((2, n_z)),
            dma((2, 4 * n_z)),
            dma((2, 2)),
            dma((2, GROUP)),
            dma((2, GROUP)),
            dma((2, n_group)),
            dma((2, GROUP)),
            dma((2, GROUP)),
        ],
        compiler_params=pltpu.CompilerParams(
            collective_id=0, has_side_effects=True, vmem_limit_bytes=56 * 1024 * 1024
        ),
    )(
        features.reshape(rows // blk, blk, width),
        tile_values,
        tile_row,
        tile_col,
        tile_count,
        weight,
        bias.reshape(1, wide),
        cotangent,
    )
    shapes = [jax.ShapeDtypeStruct(x.shape, x.dtype) for x in (hidden, weight_grad, bias_grad)]
    hidden, weight_grad, bias_grad = pl.pallas_call(
        hand_over,
        out_shape=shapes,
        in_specs=[anywhere] * 3,
        out_specs=[anywhere] * 3,
        scratch_shapes=[pltpu.VMEM(x.shape, x.dtype) for x in shapes] + [dma((3,)), dma((3,))],
        compiler_params=pltpu.CompilerParams(vmem_limit_bytes=60 * 1024 * 1024),
    )(hidden, weight_grad, bias_grad)
    return (hidden, weight_grad, bias_grad.reshape(wide))


def solution(mesh):
    in_specs = (
        P(("team", "row"), None),
        P(("team", "row"), None, None, None),
        P(("team", "row"), None),
        P(("team", "row"), None),
        P(("team", "row")),
        P(),
        P(),
        P(("team", "row"), None),
    )
    out_specs = (P(("team", "row"), None), P(), P())
    return jax.shard_map(
        functools.partial(local, mesh.shape["row"]),
        mesh=mesh,
        in_specs=in_specs,
        out_specs=out_specs,
        check_vma=False,
    )
```

```python
import functools

import jax
import jax.numpy as jnp
from jax import lax
from jax.experimental import pallas as pl
from jax.experimental.pallas import tpu as pltpu
from jax.sharding import PartitionSpec as P

MESH = pl.DeviceIdType.MESH
GROUP = 16
LANES = 128


def gelu_parts(values):
    gelu_coef = 0.7978845608
    tangent_h = jnp.tanh(gelu_coef * (values + 0.044715 * values * values * values))
    result = 0.5 * values * (1.0 + tangent_h)
    derive = 0.5 * (1.0 + tangent_h) + 0.5 * values * (1.0 - tangent_h * tangent_h) * gelu_coef * (
        1.0 + 3.0 * 0.044715 * values * values
    )
    return (result, derive)


def flip(value, bits):
    result = value
    weight = 1
    while weight <= bits:
        if bits & weight:
            bit = lax.rem(lax.div(value, weight), 2)
            result = result + weight * (1 - 2 * bit)
        weight *= 2
    return result


def kernel(
    n_row,
    features,
    tile_values,
    tile_row,
    tile_col,
    tile_count,
    weight,
    bias,
    cotangent,
    hidden_out,
    weight_out,
    bias_out,
    near,
    near_other,
    far,
    far_other,
    tiles,
    weight_v,
    bias_v,
    cot_v,
    hidden_v,
    total,
    part,
    pair,
    red,
    scattered,
    bias_in,
    owned,
    crossed,
    fin,
    fin_other,
    wg,
    bg,
    local_sem,
    tile_sem,
    z_sem,
    x_sem,
    y_sem,
    xd_sem,
    yd_sem,
    core_sem,
    pair_sem,
    rs_sem,
    rb_sem,
    cross_sem,
    ag_sem,
    ab_sem,
):
    team, row = lax.axis_index("team"), lax.axis_index("row")
    a, core = lax.div(team, 2), lax.rem(team, 2)
    z, b = lax.div(row, 2), lax.rem(row, 2)
    n_z = n_row // 2
    slots = tile_values.shape[1]
    blk = tile_values.shape[2]

    x_dev = ((1 - a) * 2 + core, row)
    y_dev = (team, z * 2 + (1 - b))
    c_dev = (a * 2 + (1 - core), row)

    def rows_of(z_now, b_now):
        return pl.ds(2 * (z_now * 2 + b_now), 2)

    own = rows_of(z, b)
    load_own = pltpu.make_async_copy(features, near.at[own], local_sem.at[0])
    load_own.start()
    panels = [a * 2 + core, a * 2 + 1 - core, (1 - a) * 2 + core, (1 - a) * 2 + 1 - core]
    loads = [
        pltpu.make_async_copy(weight, weight_v, local_sem.at[1]),
        pltpu.make_async_copy(bias, bias_v, local_sem.at[2]),
        pltpu.make_async_copy(cotangent, cot_v, local_sem.at[3]),
    ]
    tile_loads = [
        pltpu.make_async_copy(tile_values.at[panel], tiles.at[i], tile_sem.at[i])
        for i, panel in enumerate(panels)
    ]

    empty = 2 * n_row
    for ref in (near, near_other, far, far_other):
        ref[empty] = jnp.zeros((blk, LANES), jnp.bfloat16)

    barrier = pltpu.get_barrier_semaphore()
    greeted = [c_dev]
    for i in range(1, 2 * n_row):
        flat = lax.rem(a * n_row + row + i, 2 * n_row)
        greeted.append((lax.div(flat, n_row) * 2 + core, lax.rem(flat, n_row)))
    for dev in greeted:
        pl.semaphore_signal(barrier, inc=1, device_id=dev, device_id_type=MESH)
    pl.semaphore_wait(barrier, len(greeted))
    load_own.wait()

    sent = []

    def remote(src, dst, sems, i, dev):
        return pltpu.make_async_remote_copy(
            src_ref=src,
            dst_ref=dst,
            send_sem=sems.at[0, i],
            recv_sem=sems.at[1, i],
            device_id=dev,
            device_id_type=MESH,
        )

    def send(src, dst, sems, i, dev):
        copy = remote(src, dst, sems, i, dev)
        copy.start()
        return copy

    def arrived(ref, sems, i, dev):
        remote(ref, ref, sems, i, dev).wait_recv()

    def full(source):
        rows = rows_of(source, b)
        send(near.at[rows], near.at[rows], y_sem, source, y_dev)
        send(near.at[rows], far.at[rows], x_sem, source, x_dev)
        send(near.at[rows], near_other.at[rows], core_sem, source, c_dev)

    def pass_on(source, way):
        rows = rows_of(source, b)
        dev = (team, (z + 1 - 2 * way) * 2 + b)

        def copy():
            return remote(near.at[rows], near.at[rows], z_sem, way * n_z + source, dev)

        @pl.when(z < n_z - 1 if way == 0 else z > 0)
        def _():
            copy().start()

    def diagonal(source):
        mine, other = rows_of(source, b), rows_of(source, 1 - b)
        arrived(near.at[other], y_sem, source, y_dev)
        second = 2 * (source * 2 + 1 - b) + 1
        send(near.at[second], far.at[second], xd_sem, source, x_dev)
        send(near.at[other], near_other.at[other], core_sem, n_z + source, c_dev)
        arrived(far.at[mine], x_sem, source, x_dev)
        first = 2 * (source * 2 + b)
        send(far.at[first], far.at[first], yd_sem, source, y_dev)
        send(far.at[mine], far_other.at[mine], core_sem, 2 * n_z + source, c_dev)

    def last(source):
        other = rows_of(source, 1 - b)
        first = 2 * (source * 2 + 1 - b)
        arrived(far.at[first + 1], xd_sem, source, x_dev)
        arrived(far.at[first], yd_sem, source, y_dev)
        send(far.at[other], far_other.at[other], core_sem, 3 * n_z + source, c_dev)

    def both_ways(t, act):
        for way in range(2):
            source = z - t if way == 0 else z + t

            @pl.when(source >= 0 if way == 0 else source < n_z)
            def _():
                act(source, way)

    def receive(source, way):
        rows = rows_of(source, b)
        dev = (team, (z - 1 + 2 * way) * 2 + b)
        arrived(near.at[rows], z_sem, way * n_z + source, dev)
        pass_on(source, way)
        full(source)

    def from_core(ref, first, b_now):
        for j in range(n_z):
            arrived(ref.at[rows_of(j, b_now)], core_sem, first * n_z + j, c_dev)

    def all_sent():
        for way in range(2):
            for source in range(n_z):
                goes = (z < n_z - 1) & (z >= source) if way == 0 else (z > 0) & (z <= source)
                rows = rows_of(source, b)

                @pl.when(goes)
                def _():
                    remote(near.at[rows], near.at[rows], z_sem, way * n_z + source, c_dev).wait_send()

        for source in range(n_z):
            rows = rows_of(source, b)
            for sems in (y_sem, x_sem):
                remote(near.at[rows], near.at[rows], sems, source, c_dev).wait_send()
            for sems in (xd_sem, yd_sem):
                one = near.at[2 * source]
                remote(one, one, sems, source, c_dev).wait_send()
            for kind in range(4):
                remote(near.at[rows], near.at[rows], core_sem, kind * n_z + source, c_dev).wait_send()

    def aggregate(i, feats):
        tile_loads[i].wait()
        panel = panels[i]
        count = tile_count[panel]
        step = 4 if slots % 4 == 0 else slots

        def add(base, carry):
            left, right = [], []
            for k in range(step):
                s = base * step + k
                col = tile_col[panel, s]
                live = s < count
                place = tile_row[panel, s]
                upper = feats[jnp.where(live & (place == 0), col, empty)]
                lower = feats[jnp.where(live & (place == 1), col, empty)]
                left.append(tiles[i, s])
                right.append(jnp.concatenate([upper, lower], axis=1))
            total[...] += jnp.dot(
                jnp.concatenate(left, axis=1),
                jnp.concatenate(right, axis=0),
                preferred_element_type=jnp.float32,
            )
            return carry

        lax.fori_loop(0, slots // step, add, 0)

    pass_on(z, 0)
    pass_on(z, 1)
    full(z)
    for copy in tile_loads + loads:
        copy.start()
    total[...] = jnp.zeros_like(total)
    wg[...] = jnp.zeros_like(wg)
    bg[...] = jnp.zeros_like(bg)
    for t in range(1, n_z):
        both_ways(t, receive)
        if t == 1:
            diagonal(z)
        else:
            both_ways(t - 1, lambda source, way: diagonal(source))
    both_ways(n_z - 1, lambda source, way: diagonal(source))
    aggregate(0, near)
    last(z)
    for t in range(1, n_z // 2):
        both_ways(t, lambda source, way: last(source))
    from_core(near_other, 0, b)
    from_core(near_other, 1, 1 - b)
    aggregate(1, near_other)
    for t in range(n_z // 2, n_z):
        both_ways(t, lambda source, way: last(source))
    aggregate(2, far)
    from_core(far_other, 2, b)
    from_core(far_other, 3, 1 - b)
    aggregate(3, far_other)

    for copy in loads:
        copy.wait()
    step = 128
    for h in range(2):

        def layer(k, carry):
            inner = pl.ds(pl.multiple_of(k * step, step), step)
            outer = pl.ds(pl.multiple_of(h * blk + k * step, step), step)
            agg = total[inner, h * LANES : (h + 1) * LANES].astype(jnp.bfloat16)
            pre = jnp.dot(agg, weight_v[...], preferred_element_type=jnp.float32) + bias_v[...]
            result, derive = gelu_parts(pre)
            hidden_v[outer, :] = result.astype(jnp.bfloat16)
            slope = cot_v[outer, :].astype(jnp.float32) * derive
            wg[...] += lax.dot_general(
                agg,
                slope.astype(jnp.bfloat16),
                (((0,), (0,)), ((), ())),
                preferred_element_type=jnp.float32,
            )
            bg[...] += jnp.sum(slope, axis=0, keepdims=True)
            return carry

        lax.fori_loop(0, blk // step, layer, 0)
    weight_part, bias_part = wg[...], bg[...]
    for h in range(2):
        lanes = slice(h * LANES, (h + 1) * LANES)
        part[h, 0:GROUP] = weight_part[:, lanes].reshape(GROUP, 8, LANES)
        part[h, GROUP] = jnp.broadcast_to(bias_part[:, lanes], (8, LANES))
    store_hidden = pltpu.make_async_copy(hidden_v, hidden_out, local_sem.at[0])
    store_hidden.start()

    sent.append(send(part.at[1 - core], pair, pair_sem, 0, c_dev))
    arrived(pair, pair_sem, 0, c_dev)
    red[...] = part[core] + pair[...]

    group, member = lax.div(row, 8), a * 8 + lax.rem(row, 8)

    def at(member_now, group_now):
        return (lax.div(member_now, 8) * 2 + core, group_now * 8 + lax.rem(member_now, 8))

    head = at(0, group)
    def loop(act):
        def body(i, carry):
            act(i)
            return carry

        lax.fori_loop(1, GROUP, body, 0)

    def scatter(i):
        peer = lax.rem(member + i, GROUP)
        return remote(red.at[peer], scattered.at[member], rs_sem, i, at(peer, group))

    loop(lambda i: scatter(i).start())

    @pl.when(member != 0)
    def _():
        copy = pltpu.make_async_remote_copy(
            src_ref=red.at[GROUP],
            dst_ref=bias_in.at[member],
            send_sem=rb_sem.at[0, 0],
            recv_sem=rb_sem.at[1, member],
            device_id=head,
            device_id_type=MESH,
        )
        copy.start()
        copy.wait_send()

    scattered[member] = red[member]
    owned[1] = jnp.zeros((8, LANES), jnp.float32)
    def from_peer(ref, sems, i):
        peer = lax.rem(member + GROUP - i, GROUP)
        arrived(ref.at[peer], sems, i, at(peer, group))

    loop(lambda i: from_peer(scattered, rs_sem, i))
    owned[0] = jnp.sum(scattered[...], axis=0)

    @pl.when(member == 0)
    def _():
        bias_in[0] = red[GROUP]
        loop(lambda i: remote(bias_in.at[i], bias_in.at[i], rb_sem, i, c_dev).wait_recv())
        owned[1] = jnp.sum(bias_in[...], axis=0)

    n_group = n_row // 8
    if n_group > 1:
        for g in range(1, n_group):
            dev = at(member, lax.rem(group + g, n_group))
            sent.append(send(owned, crossed.at[g], cross_sem, g, dev))
        crossed[0] = owned[...]
        for g in range(1, n_group):
            arrived(crossed.at[g], cross_sem, g, at(member, lax.rem(group + n_group - g, n_group)))
        for g in range(1, n_group):
            sent.pop().wait_send()
        ordered = jnp.zeros(owned.shape, jnp.float32)
        for g in range(n_group):
            ordered = ordered + crossed[lax.rem(group + n_group - g, n_group)]
        owned[...] = ordered

    def spread(i):
        peer = lax.rem(member + i, GROUP)
        return remote(owned.at[0], fin.at[member], ag_sem, i, at(peer, group))

    loop(lambda i: spread(i).start())

    @pl.when(member == 0)
    def _():
        def spread_bias(i):
            return remote(owned.at[1], fin.at[GROUP], ab_sem, i, at(i, group))

        loop(lambda i: spread_bias(i).start())
        fin[GROUP] = owned[1]
        loop(lambda i: spread_bias(i).wait_send())

    @pl.when(member != 0)
    def _():
        pltpu.make_async_remote_copy(
            src_ref=owned.at[1],
            dst_ref=fin.at[GROUP],
            send_sem=ab_sem.at[0, 0],
            recv_sem=ab_sem.at[1, member],
            device_id=head,
            device_id_type=MESH,
        ).wait_recv()

    fin[member] = owned[0]
    loop(lambda i: from_peer(fin, ag_sem, i))
    sent.append(send(fin, fin_other, pair_sem, 1, c_dev))
    arrived(fin_other, pair_sem, 1, c_dev)
    mine, other = fin[...], fin_other[...]
    for h in range(2):
        half = jnp.where(core == h, mine, other)
        lanes = slice(h * LANES, (h + 1) * LANES)
        weight_out[:, lanes] = half[0:GROUP].reshape(GROUP * 8, LANES)
        bias_out[:, lanes] = half[GROUP, 0:1]
    for copy in sent:
        copy.wait_send()
    loop(lambda i: scatter(i).wait_send())
    loop(lambda i: spread(i).wait_send())
    all_sent()
    store_hidden.wait()


def hand_over(*refs):
    ins, outs, held, load_sem, store_sem = refs[0:3], refs[3:6], refs[6:9], refs[9], refs[10]
    loads = [pltpu.make_async_copy(ins[i], held[i], load_sem.at[i]) for i in range(3)]
    stores = [pltpu.make_async_copy(held[i], outs[i], store_sem.at[i]) for i in range(3)]
    for copy in loads:
        copy.start()
    for load, store in zip(loads, stores):
        load.wait()
        store.start()
    for copy in stores:
        copy.wait()


def local(n_row, features, tile_values, tile_row, tile_col, tile_count, weight, bias, cotangent):
    n_panel, slots, blk, _ = tile_values.shape
    rows, width = features.shape
    wide = weight.shape[1]
    n_z = n_row // 2
    n_group = n_row // 8
    dma = pltpu.SemaphoreType.DMA
    anywhere = pl.BlockSpec(memory_space=pl.ANY)
    smem = pl.BlockSpec(memory_space=pltpu.SMEM)
    vmem = pl.BlockSpec(memory_space=pltpu.VMEM)
    hidden, weight_grad, bias_grad = pl.pallas_call(
        functools.partial(kernel, n_row),
        out_shape=[
            jax.ShapeDtypeStruct((rows, wide), jnp.bfloat16),
            jax.ShapeDtypeStruct((width, wide), jnp.float32),
            jax.ShapeDtypeStruct((1, wide), jnp.float32),
        ],
        in_specs=[anywhere, anywhere, smem, smem, smem, anywhere, anywhere, anywhere],
        out_specs=[anywhere, vmem, vmem],
        scratch_shapes=[
            pltpu.VMEM((2 * n_row + 1, blk, width), jnp.bfloat16),
            pltpu.VMEM((2 * n_row + 1, blk, width), jnp.bfloat16),
            pltpu.VMEM((2 * n_row + 1, blk, width), jnp.bfloat16),
            pltpu.VMEM((2 * n_row + 1, blk, width), jnp.bfloat16),
            pltpu.VMEM((n_panel, slots, blk, blk), jnp.bfloat16),
            pltpu.VMEM((width, wide), jnp.bfloat16),
            pltpu.VMEM((1, wide), jnp.float32),
            pltpu.VMEM((rows, wide), jnp.bfloat16),
            pltpu.VMEM((rows, wide), jnp.bfloat16),
            pltpu.VMEM((blk, 2 * width), jnp.float32),
            pltpu.VMEM((2, GROUP + 1, 8, LANES), jnp.float32),
            pltpu.VMEM((GROUP + 1, 8, LANES), jnp.float32),
            pltpu.VMEM((GROUP + 1, 8, LANES), jnp.float32),
            pltpu.VMEM((GROUP, 8, LANES), jnp.float32),
            pltpu.VMEM((GROUP, 8, LANES), jnp.float32),
            pltpu.VMEM((2, 8, LANES), jnp.float32),
            pltpu.VMEM((n_group, 2, 8, LANES), jnp.float32),
            pltpu.VMEM((GROUP + 1, 8, LANES), jnp.float32),
            pltpu.VMEM((GROUP + 1, 8, LANES), jnp.float32),
            pltpu.VMEM((width, wide), jnp.float32),
            pltpu.VMEM((1, wide), jnp.float32),
            dma((4,)),
            dma((4,)),
            dma((2, 2 * n_z)),
            dma((2, n_z)),
            dma((2, n_z)),
            dma((2, n_z)),
            dma((2, n_z)),
            dma((2, 4 * n_z)),
            dma((2, 2)),
            dma((2, GROUP)),
            dma((2, GROUP)),
            dma((2, n_group)),
            dma((2, GROUP)),
            dma((2, GROUP)),
        ],
        compiler_params=pltpu.CompilerParams(
            collective_id=0, has_side_effects=True, vmem_limit_bytes=56 * 1024 * 1024
        ),
    )(
        features.reshape(rows // blk, blk, width),
        tile_values,
        tile_row,
        tile_col,
        tile_count,
        weight,
        bias.reshape(1, wide),
        cotangent,
    )
    shapes = [jax.ShapeDtypeStruct(x.shape, x.dtype) for x in (hidden, weight_grad, bias_grad)]
    hidden, weight_grad, bias_grad = pl.pallas_call(
        hand_over,
        out_shape=shapes,
        in_specs=[anywhere] * 3,
        out_specs=[anywhere] * 3,
        scratch_shapes=[pltpu.VMEM(x.shape, x.dtype) for x in shapes] + [dma((3,)), dma((3,))],
        compiler_params=pltpu.CompilerParams(vmem_limit_bytes=60 * 1024 * 1024),
    )(hidden, weight_grad, bias_grad)
    return (hidden, weight_grad, bias_grad.reshape(wide))


def solution(mesh):
    in_specs = (
        P(("team", "row"), None),
        P(("team", "row"), None, None, None),
        P(("team", "row"), None),
        P(("team", "row"), None),
        P(("team", "row")),
        P(),
        P(),
        P(("team", "row"), None),
    )
    out_specs = (P(("team", "row"), None), P(), P())
    return jax.shard_map(
        functools.partial(local, mesh.shape["row"]),
        mesh=mesh,
        in_specs=in_specs,
        out_specs=out_specs,
        check_vma=False,
    )
```

```python
import functools

import jax
import jax.numpy as jnp
from jax import lax
from jax.experimental import pallas as pl
from jax.experimental.pallas import tpu as pltpu
from jax.sharding import PartitionSpec as P

MESH = pl.DeviceIdType.MESH
GROUP = 16
LANES = 128


def gelu_parts(values):
    gelu_coef = 0.7978845608
    tangent_h = jnp.tanh(gelu_coef * (values + 0.044715 * values * values * values))
    result = 0.5 * values * (1.0 + tangent_h)
    derive = 0.5 * (1.0 + tangent_h) + 0.5 * values * (1.0 - tangent_h * tangent_h) * gelu_coef * (
        1.0 + 3.0 * 0.044715 * values * values
    )
    return (result, derive)


def flip(value, bits):
    result = value
    weight = 1
    while weight <= bits:
        if bits & weight:
            bit = lax.rem(lax.div(value, weight), 2)
            result = result + weight * (1 - 2 * bit)
        weight *= 2
    return result


def kernel(
    n_row,
    features,
    tile_values,
    tile_row,
    tile_col,
    tile_count,
    weight,
    bias,
    cotangent,
    hidden_out,
    weight_out,
    bias_out,
    near,
    near_other,
    far,
    far_other,
    tiles,
    weight_v,
    bias_v,
    cot_v,
    hidden_v,
    total,
    part,
    pair,
    red,
    scattered,
    bias_in,
    owned,
    crossed,
    fin,
    fin_other,
    wg,
    bg,
    local_sem,
    tile_sem,
    z_sem,
    x_sem,
    y_sem,
    xd_sem,
    yd_sem,
    core_sem,
    pair_sem,
    rs_sem,
    rb_sem,
    cross_sem,
    ag_sem,
    ab_sem,
):
    team, row = lax.axis_index("team"), lax.axis_index("row")
    a, core = lax.div(team, 2), lax.rem(team, 2)
    z, b = lax.div(row, 2), lax.rem(row, 2)
    n_z = n_row // 2
    slots = tile_values.shape[1]
    blk = tile_values.shape[2]

    x_dev = ((1 - a) * 2 + core, row)
    y_dev = (team, z * 2 + (1 - b))
    c_dev = (a * 2 + (1 - core), row)

    def rows_of(z_now, b_now):
        return pl.ds(2 * (z_now * 2 + b_now), 2)

    own = rows_of(z, b)
    load_own = pltpu.make_async_copy(features, near.at[own], local_sem.at[0])
    load_own.start()
    panels = [a * 2 + core, a * 2 + 1 - core, (1 - a) * 2 + core, (1 - a) * 2 + 1 - core]
    loads = [
        pltpu.make_async_copy(weight, weight_v, local_sem.at[1]),
        pltpu.make_async_copy(bias, bias_v, local_sem.at[2]),
        pltpu.make_async_copy(cotangent, cot_v, local_sem.at[3]),
    ]
    tile_loads = [
        pltpu.make_async_copy(tile_values.at[panel], tiles.at[i], tile_sem.at[i])
        for i, panel in enumerate(panels)
    ]

    empty = 2 * n_row
    for ref in (near, near_other, far, far_other):
        ref[empty] = jnp.zeros((blk, LANES), jnp.bfloat16)

    barrier = pltpu.get_barrier_semaphore()
    greeted = [c_dev]
    for i in range(1, 2 * n_row):
        flat = lax.rem(a * n_row + row + i, 2 * n_row)
        greeted.append((lax.div(flat, n_row) * 2 + core, lax.rem(flat, n_row)))
    for dev in greeted:
        pl.semaphore_signal(barrier, inc=1, device_id=dev, device_id_type=MESH)
    pl.semaphore_wait(barrier, len(greeted))
    load_own.wait()

    sent = []

    def remote(src, dst, sems, i, dev):
        return pltpu.make_async_remote_copy(
            src_ref=src,
            dst_ref=dst,
            send_sem=sems.at[0, i],
            recv_sem=sems.at[1, i],
            device_id=dev,
            device_id_type=MESH,
        )

    def send(src, dst, sems, i, dev):
        copy = remote(src, dst, sems, i, dev)
        copy.start()
        return copy

    def arrived(ref, sems, i, dev):
        remote(ref, ref, sems, i, dev).wait_recv()

    def spot(source, b_now, h):
        return 2 * (source * 2 + b_now) + h

    def full(source, h):
        one = near.at[spot(source, b, h)]
        ways = [(y_sem, near, y_dev), (x_sem, far, x_dev)]
        for sems, ref, dev in ways if h == 1 else ways[::-1]:
            send(one, ref.at[spot(source, b, h)], sems, 2 * source + h, dev)

    def to_core(ref, ref_other, kind, source, b_now):
        rows = rows_of(source, b_now)
        send(ref.at[rows], ref_other.at[rows], core_sem, kind * n_z + source, c_dev)

    def pass_on(source, way, h):
        one = near.at[spot(source, b, h)]
        dev = (team, (z + 1 - 2 * way) * 2 + b)

        @pl.when(z < n_z - 1 if way == 0 else z > 0)
        def _():
            remote(one, one, z_sem, 2 * (way * n_z + source) + h, dev).start()

    def cross(source):
        first, second = spot(source, b, 0), spot(source, 1 - b, 1)
        arrived(far.at[first], x_sem, 2 * source, x_dev)
        send(far.at[first], far.at[first], yd_sem, source, y_dev)
        arrived(near.at[second], y_sem, 2 * source + 1, y_dev)
        send(near.at[second], far.at[second], xd_sem, source, x_dev)

    def share(source):
        arrived(near.at[spot(source, 1 - b, 0)], y_sem, 2 * source, y_dev)
        to_core(near, near_other, 1, source, 1 - b)
        arrived(far.at[spot(source, b, 1)], x_sem, 2 * source + 1, x_dev)
        to_core(far, far_other, 2, source, b)

    def last(source):
        other = rows_of(source, 1 - b)
        first = 2 * (source * 2 + 1 - b)
        arrived(far.at[first + 1], xd_sem, source, x_dev)
        arrived(far.at[first], yd_sem, source, y_dev)
        send(far.at[other], far_other.at[other], core_sem, 3 * n_z + source, c_dev)

    def both_ways(t, act):
        for way in range(2):
            source = z - t if way == 0 else z + t

            @pl.when(source >= 0 if way == 0 else source < n_z)
            def _():
                act(source, way)

    def receive(source, way):
        dev = (team, (z - 1 + 2 * way) * 2 + b)
        for h in range(2):
            arrived(near.at[spot(source, b, h)], z_sem, 2 * (way * n_z + source) + h, dev)
            pass_on(source, way, h)
            full(source, h)
        to_core(near, near_other, 0, source, b)

    def from_core(ref, first, b_now):
        for j in range(n_z):
            arrived(ref.at[rows_of(j, b_now)], core_sem, first * n_z + j, c_dev)

    def all_sent():
        for way in range(2):
            for source in range(n_z):
                goes = (z < n_z - 1) & (z >= source) if way == 0 else (z > 0) & (z <= source)
                one = near.at[spot(source, b, 0)]

                @pl.when(goes)
                def _():
                    for h in range(2):
                        i = 2 * (way * n_z + source) + h
                        remote(one, one, z_sem, i, c_dev).wait_send()

        for source in range(n_z):
            rows = rows_of(source, b)
            one = near.at[spot(source, b, 0)]
            for sems in (y_sem, x_sem):
                for h in range(2):
                    remote(one, one, sems, 2 * source + h, c_dev).wait_send()
            for sems in (xd_sem, yd_sem):
                remote(one, one, sems, source, c_dev).wait_send()
            for kind in range(4):
                remote(near.at[rows], near.at[rows], core_sem, kind * n_z + source, c_dev).wait_send()

    def aggregate(i, feats):
        tile_loads[i].wait()
        panel = panels[i]
        count = tile_count[panel]
        step = 4 if slots % 4 == 0 else slots

        def add(base, carry):
            left, right = [], []
            for k in range(step):
                s = base * step + k
                col = tile_col[panel, s]
                live = s < count
                place = tile_row[panel, s]
                upper = feats[jnp.where(live & (place == 0), col, empty)]
                lower = feats[jnp.where(live & (place == 1), col, empty)]
                left.append(tiles[i, s])
                right.append(jnp.concatenate([upper, lower], axis=1))
            total[...] += jnp.dot(
                jnp.concatenate(left, axis=1),
                jnp.concatenate(right, axis=0),
                preferred_element_type=jnp.float32,
            )
            return carry

        lax.fori_loop(0, slots // step, add, 0)

    for h in range(2):
        pass_on(z, 0, h)
        pass_on(z, 1, h)
        full(z, h)
    to_core(near, near_other, 0, z, b)
    for copy in tile_loads + loads:
        copy.start()
    total[...] = jnp.zeros_like(total)
    wg[...] = jnp.zeros_like(wg)
    bg[...] = jnp.zeros_like(bg)
    def step_of(act, t):
        if t == 0:
            act(z)
        else:
            both_ways(t, lambda source, way: act(source))

    for t in range(1, n_z):
        both_ways(t, receive)
        step_of(cross, t - 1)
        if t > 1:
            step_of(share, t - 2)
    step_of(cross, n_z - 1)
    step_of(share, n_z - 2)
    step_of(share, n_z - 1)
    aggregate(0, near)
    last(z)
    for t in range(1, n_z // 2):
        both_ways(t, lambda source, way: last(source))
    from_core(near_other, 0, b)
    from_core(near_other, 1, 1 - b)
    aggregate(1, near_other)
    for t in range(n_z // 2, n_z):
        both_ways(t, lambda source, way: last(source))
    aggregate(2, far)
    from_core(far_other, 2, b)
    from_core(far_other, 3, 1 - b)
    aggregate(3, far_other)

    for copy in loads:
        copy.wait()
    step = 128
    for h in range(2):

        def layer(k, carry):
            inner = pl.ds(pl.multiple_of(k * step, step), step)
            outer = pl.ds(pl.multiple_of(h * blk + k * step, step), step)
            agg = total[inner, h * LANES : (h + 1) * LANES].astype(jnp.bfloat16)
            pre = jnp.dot(agg, weight_v[...], preferred_element_type=jnp.float32) + bias_v[...]
            result, derive = gelu_parts(pre)
            hidden_v[outer, :] = result.astype(jnp.bfloat16)
            slope = cot_v[outer, :].astype(jnp.float32) * derive
            wg[...] += lax.dot_general(
                agg,
                slope.astype(jnp.bfloat16),
                (((0,), (0,)), ((), ())),
                preferred_element_type=jnp.float32,
            )
            bg[...] += jnp.sum(slope, axis=0, keepdims=True)
            return carry

        lax.fori_loop(0, blk // step, layer, 0)
    weight_part, bias_part = wg[...], bg[...]
    for h in range(2):
        lanes = slice(h * LANES, (h + 1) * LANES)
        part[h, 0:GROUP] = weight_part[:, lanes].reshape(GROUP, 8, LANES)
        part[h, GROUP] = jnp.broadcast_to(bias_part[:, lanes], (8, LANES))
    store_hidden = pltpu.make_async_copy(hidden_v, hidden_out, local_sem.at[0])
    store_hidden.start()

    sent.append(send(part.at[1 - core], pair, pair_sem, 0, c_dev))
    arrived(pair, pair_sem, 0, c_dev)
    red[...] = part[core] + pair[...]

    group, member = lax.div(row, 8), a * 8 + lax.rem(row, 8)

    def at(member_now, group_now):
        return (lax.div(member_now, 8) * 2 + core, group_now * 8 + lax.rem(member_now, 8))

    head = at(0, group)
    def loop(act):
        def body(i, carry):
            act(i)
            return carry

        lax.fori_loop(1, GROUP, body, 0)

    def scatter(i):
        peer = lax.rem(member + i, GROUP)
        return remote(red.at[peer], scattered.at[member], rs_sem, i, at(peer, group))

    loop(lambda i: scatter(i).start())

    @pl.when(member != 0)
    def _():
        copy = pltpu.make_async_remote_copy(
            src_ref=red.at[GROUP],
            dst_ref=bias_in.at[member],
            send_sem=rb_sem.at[0, 0],
            recv_sem=rb_sem.at[1, member],
            device_id=head,
            device_id_type=MESH,
        )
        copy.start()
        copy.wait_send()

    scattered[member] = red[member]
    owned[1] = jnp.zeros((8, LANES), jnp.float32)
    def from_peer(ref, sems, i):
        peer = lax.rem(member + GROUP - i, GROUP)
        arrived(ref.at[peer], sems, i, at(peer, group))

    loop(lambda i: from_peer(scattered, rs_sem, i))
    owned[0] = jnp.sum(scattered[...], axis=0)

    @pl.when(member == 0)
    def _():
        bias_in[0] = red[GROUP]
        loop(lambda i: remote(bias_in.at[i], bias_in.at[i], rb_sem, i, c_dev).wait_recv())
        owned[1] = jnp.sum(bias_in[...], axis=0)

    n_group = n_row // 8
    if n_group > 1:
        for g in range(1, n_group):
            dev = at(member, lax.rem(group + g, n_group))
            sent.append(send(owned, crossed.at[g], cross_sem, g, dev))
        crossed[0] = owned[...]
        for g in range(1, n_group):
            arrived(crossed.at[g], cross_sem, g, at(member, lax.rem(group + n_group - g, n_group)))
        for g in range(1, n_group):
            sent.pop().wait_send()
        ordered = jnp.zeros(owned.shape, jnp.float32)
        for g in range(n_group):
            ordered = ordered + crossed[lax.rem(group + n_group - g, n_group)]
        owned[...] = ordered

    def spread(i):
        peer = lax.rem(member + i, GROUP)
        return remote(owned.at[0], fin.at[member], ag_sem, i, at(peer, group))

    loop(lambda i: spread(i).start())

    @pl.when(member == 0)
    def _():
        def spread_bias(i):
            return remote(owned.at[1], fin.at[GROUP], ab_sem, i, at(i, group))

        loop(lambda i: spread_bias(i).start())
        fin[GROUP] = owned[1]
        loop(lambda i: spread_bias(i).wait_send())

    @pl.when(member != 0)
    def _():
        pltpu.make_async_remote_copy(
            src_ref=owned.at[1],
            dst_ref=fin.at[GROUP],
            send_sem=ab_sem.at[0, 0],
            recv_sem=ab_sem.at[1, member],
            device_id=head,
            device_id_type=MESH,
        ).wait_recv()

    fin[member] = owned[0]
    loop(lambda i: from_peer(fin, ag_sem, i))
    sent.append(send(fin, fin_other, pair_sem, 1, c_dev))
    arrived(fin_other, pair_sem, 1, c_dev)
    mine, other = fin[...], fin_other[...]
    for h in range(2):
        half = jnp.where(core == h, mine, other)
        lanes = slice(h * LANES, (h + 1) * LANES)
        weight_out[:, lanes] = half[0:GROUP].reshape(GROUP * 8, LANES)
        bias_out[:, lanes] = half[GROUP, 0:1]
    for copy in sent:
        copy.wait_send()
    loop(lambda i: scatter(i).wait_send())
    loop(lambda i: spread(i).wait_send())
    all_sent()
    store_hidden.wait()


def hand_over(*refs):
    ins, outs, held, load_sem, store_sem = refs[0:3], refs[3:6], refs[6:9], refs[9], refs[10]
    loads = [pltpu.make_async_copy(ins[i], held[i], load_sem.at[i]) for i in range(3)]
    stores = [pltpu.make_async_copy(held[i], outs[i], store_sem.at[i]) for i in range(3)]
    for copy in loads:
        copy.start()
    for load, store in zip(loads, stores):
        load.wait()
        store.start()
    for copy in stores:
        copy.wait()


def local(n_row, features, tile_values, tile_row, tile_col, tile_count, weight, bias, cotangent):
    n_panel, slots, blk, _ = tile_values.shape
    rows, width = features.shape
    wide = weight.shape[1]
    n_z = n_row // 2
    n_group = n_row // 8
    dma = pltpu.SemaphoreType.DMA
    anywhere = pl.BlockSpec(memory_space=pl.ANY)
    smem = pl.BlockSpec(memory_space=pltpu.SMEM)
    vmem = pl.BlockSpec(memory_space=pltpu.VMEM)
    hidden, weight_grad, bias_grad = pl.pallas_call(
        functools.partial(kernel, n_row),
        out_shape=[
            jax.ShapeDtypeStruct((rows, wide), jnp.bfloat16),
            jax.ShapeDtypeStruct((width, wide), jnp.float32),
            jax.ShapeDtypeStruct((1, wide), jnp.float32),
        ],
        in_specs=[anywhere, anywhere, smem, smem, smem, anywhere, anywhere, anywhere],
        out_specs=[anywhere, vmem, vmem],
        scratch_shapes=[
            pltpu.VMEM((2 * n_row + 1, blk, width), jnp.bfloat16),
            pltpu.VMEM((2 * n_row + 1, blk, width), jnp.bfloat16),
            pltpu.VMEM((2 * n_row + 1, blk, width), jnp.bfloat16),
            pltpu.VMEM((2 * n_row + 1, blk, width), jnp.bfloat16),
            pltpu.VMEM((n_panel, slots, blk, blk), jnp.bfloat16),
            pltpu.VMEM((width, wide), jnp.bfloat16),
            pltpu.VMEM((1, wide), jnp.float32),
            pltpu.VMEM((rows, wide), jnp.bfloat16),
            pltpu.VMEM((rows, wide), jnp.bfloat16),
            pltpu.VMEM((blk, 2 * width), jnp.float32),
            pltpu.VMEM((2, GROUP + 1, 8, LANES), jnp.float32),
            pltpu.VMEM((GROUP + 1, 8, LANES), jnp.float32),
            pltpu.VMEM((GROUP + 1, 8, LANES), jnp.float32),
            pltpu.VMEM((GROUP, 8, LANES), jnp.float32),
            pltpu.VMEM((GROUP, 8, LANES), jnp.float32),
            pltpu.VMEM((2, 8, LANES), jnp.float32),
            pltpu.VMEM((n_group, 2, 8, LANES), jnp.float32),
            pltpu.VMEM((GROUP + 1, 8, LANES), jnp.float32),
            pltpu.VMEM((GROUP + 1, 8, LANES), jnp.float32),
            pltpu.VMEM((width, wide), jnp.float32),
            pltpu.VMEM((1, wide), jnp.float32),
            dma((4,)),
            dma((4,)),
            dma((2, 4 * n_z)),
            dma((2, 2 * n_z)),
            dma((2, 2 * n_z)),
            dma((2, n_z)),
            dma((2, n_z)),
            dma((2, 4 * n_z)),
            dma((2, 2)),
            dma((2, GROUP)),
            dma((2, GROUP)),
            dma((2, n_group)),
            dma((2, GROUP)),
            dma((2, GROUP)),
        ],
        compiler_params=pltpu.CompilerParams(
            collective_id=0, has_side_effects=True, vmem_limit_bytes=56 * 1024 * 1024
        ),
    )(
        features.reshape(rows // blk, blk, width),
        tile_values,
        tile_row,
        tile_col,
        tile_count,
        weight,
        bias.reshape(1, wide),
        cotangent,
    )
    shapes = [jax.ShapeDtypeStruct(x.shape, x.dtype) for x in (hidden, weight_grad, bias_grad)]
    hidden, weight_grad, bias_grad = pl.pallas_call(
        hand_over,
        out_shape=shapes,
        in_specs=[anywhere] * 3,
        out_specs=[anywhere] * 3,
        scratch_shapes=[pltpu.VMEM(x.shape, x.dtype) for x in shapes] + [dma((3,)), dma((3,))],
        compiler_params=pltpu.CompilerParams(vmem_limit_bytes=60 * 1024 * 1024),
    )(hidden, weight_grad, bias_grad)
    return (hidden, weight_grad, bias_grad.reshape(wide))


def solution(mesh):
    in_specs = (
        P(("team", "row"), None),
        P(("team", "row"), None, None, None),
        P(("team", "row"), None),
        P(("team", "row"), None),
        P(("team", "row")),
        P(),
        P(),
        P(("team", "row"), None),
    )
    out_specs = (P(("team", "row"), None), P(), P())
    return jax.shard_map(
        functools.partial(local, mesh.shape["row"]),
        mesh=mesh,
        in_specs=in_specs,
        out_specs=out_specs,
        check_vma=False,
    )
```

```python
import functools

import jax
import jax.numpy as jnp
from jax import lax
from jax.experimental import pallas as pl
from jax.experimental.pallas import tpu as pltpu
from jax.sharding import PartitionSpec as P

MESH = pl.DeviceIdType.MESH
GROUP = 16
LANES = 128


def gelu_parts(values):
    gelu_coef = 0.7978845608
    tangent_h = jnp.tanh(gelu_coef * (values + 0.044715 * values * values * values))
    result = 0.5 * values * (1.0 + tangent_h)
    derive = 0.5 * (1.0 + tangent_h) + 0.5 * values * (1.0 - tangent_h * tangent_h) * gelu_coef * (
        1.0 + 3.0 * 0.044715 * values * values
    )
    return (result, derive)


def flip(value, bits):
    result = value
    weight = 1
    while weight <= bits:
        if bits & weight:
            bit = lax.rem(lax.div(value, weight), 2)
            result = result + weight * (1 - 2 * bit)
        weight *= 2
    return result


def kernel(
    n_row,
    features,
    tile_values,
    tile_row,
    tile_col,
    tile_count,
    weight,
    bias,
    cotangent,
    hidden_out,
    weight_out,
    bias_out,
    near,
    near_other,
    far,
    far_other,
    tiles,
    weight_v,
    bias_v,
    cot_v,
    hidden_v,
    total,
    part,
    pair,
    red,
    scattered,
    bias_in,
    owned,
    crossed,
    fin,
    fin_other,
    wg,
    bg,
    local_sem,
    tile_sem,
    z_sem,
    x_sem,
    y_sem,
    xd_sem,
    yd_sem,
    zd_sem,
    core_sem,
    pair_sem,
    rs_sem,
    rb_sem,
    cross_sem,
    ag_sem,
    ab_sem,
):
    team, row = lax.axis_index("team"), lax.axis_index("row")
    a, core = lax.div(team, 2), lax.rem(team, 2)
    z, b = lax.div(row, 2), lax.rem(row, 2)
    n_z = n_row // 2
    slots = tile_values.shape[1]
    blk = tile_values.shape[2]

    x_dev = ((1 - a) * 2 + core, row)
    y_dev = (team, z * 2 + (1 - b))
    c_dev = (a * 2 + (1 - core), row)

    def rows_of(z_now, b_now):
        return pl.ds(2 * (z_now * 2 + b_now), 2)

    own = rows_of(z, b)
    load_own = pltpu.make_async_copy(features, near.at[own], local_sem.at[0])
    load_own.start()
    panels = [a * 2 + core, a * 2 + 1 - core, (1 - a) * 2 + core, (1 - a) * 2 + 1 - core]
    loads = [
        pltpu.make_async_copy(weight, weight_v, local_sem.at[1]),
        pltpu.make_async_copy(bias, bias_v, local_sem.at[2]),
        pltpu.make_async_copy(cotangent, cot_v, local_sem.at[3]),
    ]
    tile_loads = [
        pltpu.make_async_copy(tile_values.at[panel], tiles.at[i], tile_sem.at[i])
        for i, panel in enumerate(panels)
    ]

    empty = 2 * n_row
    for ref in (near, near_other, far, far_other):
        ref[empty] = jnp.zeros((blk, LANES), jnp.bfloat16)

    barrier = pltpu.get_barrier_semaphore()
    greeted = [c_dev]
    for i in range(1, 2 * n_row):
        flat = lax.rem(a * n_row + row + i, 2 * n_row)
        greeted.append((lax.div(flat, n_row) * 2 + core, lax.rem(flat, n_row)))
    for dev in greeted:
        pl.semaphore_signal(barrier, inc=1, device_id=dev, device_id_type=MESH)
    pl.semaphore_wait(barrier, len(greeted))
    load_own.wait()

    sent = []

    def remote(src, dst, sems, i, dev):
        return pltpu.make_async_remote_copy(
            src_ref=src,
            dst_ref=dst,
            send_sem=sems.at[0, i],
            recv_sem=sems.at[1, i],
            device_id=dev,
            device_id_type=MESH,
        )

    def send(src, dst, sems, i, dev):
        copy = remote(src, dst, sems, i, dev)
        copy.start()
        return copy

    def arrived(ref, sems, i, dev):
        remote(ref, ref, sems, i, dev).wait_recv()

    def spot(source, b_now, h):
        return 2 * (source * 2 + b_now) + h

    def full(source, h):
        one = near.at[spot(source, b, h)]
        ways = [(y_sem, near, y_dev), (x_sem, far, x_dev)]
        for sems, ref, dev in ways if h == 1 else ways[::-1]:
            send(one, ref.at[spot(source, b, h)], sems, 2 * source + h, dev)

    def to_core(ref, ref_other, kind, source, b_now):
        rows = rows_of(source, b_now)
        send(ref.at[rows], ref_other.at[rows], core_sem, kind * n_z + source, c_dev)

    def pass_on(source, way, h):
        one = near.at[spot(source, b, h)]
        dev = (team, (z + 1 - 2 * way) * 2 + b)

        @pl.when(z < n_z - 1 if way == 0 else z > 0)
        def _():
            remote(one, one, z_sem, 2 * (way * n_z + source) + h, dev).start()

    z_paired = flip(z, 1)
    pair_dev = (team, z_paired * 2 + b)

    def cross(source):
        first, second = spot(source, b, 0), spot(source, 1 - b, 1)
        arrived(far.at[first], x_sem, 2 * source, x_dev)

        @pl.when(source != z_paired)
        def _():
            send(far.at[first], far.at[first], yd_sem, source, y_dev)

        arrived(near.at[second], y_sem, 2 * source + 1, y_dev)

        @pl.when(source != z_paired)
        def _():
            send(near.at[second], far.at[second], xd_sem, source, x_dev)

    def share(source):
        arrived(near.at[spot(source, 1 - b, 0)], y_sem, 2 * source, y_dev)
        to_core(near, near_other, 1, source, 1 - b)
        arrived(far.at[spot(source, b, 1)], x_sem, 2 * source + 1, x_dev)
        to_core(far, far_other, 2, source, b)

    def last(source):
        other = rows_of(source, 1 - b)

        @pl.when(source != z_paired)
        def _():
            arrived(far.at[spot(source, 1 - b, 1)], xd_sem, source, x_dev)
            arrived(far.at[spot(source, 1 - b, 0)], yd_sem, source, y_dev)

        @pl.when(source == z_paired)
        def _():
            arrived(far.at[other], zd_sem, 0, pair_dev)

        to_core(far, far_other, 3, source, 1 - b)

    def hand_own():
        other = rows_of(z, 1 - b)
        arrived(far.at[spot(z, 1 - b, 1)], xd_sem, z, x_dev)
        arrived(far.at[spot(z, 1 - b, 0)], yd_sem, z, y_dev)
        send(far.at[other], far.at[other], zd_sem, 0, pair_dev)
        to_core(far, far_other, 3, z, 1 - b)

    def both_ways(t, act):
        for way in range(2):
            source = z - t if way == 0 else z + t

            @pl.when(source >= 0 if way == 0 else source < n_z)
            def _():
                act(source, way)

    def receive(source, way):
        dev = (team, (z - 1 + 2 * way) * 2 + b)
        for h in range(2):
            arrived(near.at[spot(source, b, h)], z_sem, 2 * (way * n_z + source) + h, dev)
            pass_on(source, way, h)
            full(source, h)
        to_core(near, near_other, 0, source, b)

    def from_core(ref, first, b_now):
        for j in range(n_z):
            arrived(ref.at[rows_of(j, b_now)], core_sem, first * n_z + j, c_dev)

    def all_sent():
        mine = rows_of(z, b)
        remote(far.at[mine], far.at[mine], zd_sem, 0, c_dev).wait_send()
        for way in range(2):
            for source in range(n_z):
                goes = (z < n_z - 1) & (z >= source) if way == 0 else (z > 0) & (z <= source)
                one = near.at[spot(source, b, 0)]

                @pl.when(goes)
                def _():
                    for h in range(2):
                        i = 2 * (way * n_z + source) + h
                        remote(one, one, z_sem, i, c_dev).wait_send()

        for source in range(n_z):
            rows = rows_of(source, b)
            one = near.at[spot(source, b, 0)]
            for sems in (y_sem, x_sem):
                for h in range(2):
                    remote(one, one, sems, 2 * source + h, c_dev).wait_send()

            @pl.when(source != z_paired)
            def _():
                for sems in (xd_sem, yd_sem):
                    remote(one, one, sems, source, c_dev).wait_send()

            for kind in range(4):
                remote(near.at[rows], near.at[rows], core_sem, kind * n_z + source, c_dev).wait_send()

    def aggregate(i, feats):
        tile_loads[i].wait()
        panel = panels[i]
        count = tile_count[panel]
        step = 4 if slots % 4 == 0 else slots

        def add(base, carry):
            left, right = [], []
            for k in range(step):
                s = base * step + k
                col = tile_col[panel, s]
                live = s < count
                place = tile_row[panel, s]
                upper = feats[jnp.where(live & (place == 0), col, empty)]
                lower = feats[jnp.where(live & (place == 1), col, empty)]
                left.append(tiles[i, s])
                right.append(jnp.concatenate([upper, lower], axis=1))
            total[...] += jnp.dot(
                jnp.concatenate(left, axis=1),
                jnp.concatenate(right, axis=0),
                preferred_element_type=jnp.float32,
            )
            return carry

        lax.fori_loop(0, slots // step, add, 0)

    for h in range(2):
        pass_on(z, 0, h)
        pass_on(z, 1, h)
        full(z, h)
    to_core(near, near_other, 0, z, b)
    for copy in tile_loads + loads:
        copy.start()
    total[...] = jnp.zeros_like(total)
    wg[...] = jnp.zeros_like(wg)
    bg[...] = jnp.zeros_like(bg)
    def step_of(act, t):
        if t == 0:
            act(z)
        else:
            both_ways(t, lambda source, way: act(source))

    for t in range(1, n_z):
        both_ways(t, receive)
        step_of(cross, t - 1)
        if t > 1:
            step_of(share, t - 2)
        if t == 2:
            hand_own()
    step_of(cross, n_z - 1)
    step_of(share, n_z - 2)
    step_of(share, n_z - 1)
    aggregate(0, near)
    for t in range(1, n_z // 2):
        both_ways(t, lambda source, way: last(source))
    from_core(near_other, 0, b)
    from_core(near_other, 1, 1 - b)
    aggregate(1, near_other)
    for t in range(n_z // 2, n_z):
        both_ways(t, lambda source, way: last(source))
    aggregate(2, far)
    from_core(far_other, 2, b)
    from_core(far_other, 3, 1 - b)
    aggregate(3, far_other)

    for copy in loads:
        copy.wait()
    step = 128
    for h in range(2):

        def layer(k, carry):
            inner = pl.ds(pl.multiple_of(k * step, step), step)
            outer = pl.ds(pl.multiple_of(h * blk + k * step, step), step)
            agg = total[inner, h * LANES : (h + 1) * LANES].astype(jnp.bfloat16)
            pre = jnp.dot(agg, weight_v[...], preferred_element_type=jnp.float32) + bias_v[...]
            result, derive = gelu_parts(pre)
            hidden_v[outer, :] = result.astype(jnp.bfloat16)
            slope = cot_v[outer, :].astype(jnp.float32) * derive
            wg[...] += lax.dot_general(
                agg,
                slope.astype(jnp.bfloat16),
                (((0,), (0,)), ((), ())),
                preferred_element_type=jnp.float32,
            )
            bg[...] += jnp.sum(slope, axis=0, keepdims=True)
            return carry

        lax.fori_loop(0, blk // step, layer, 0)
    weight_part, bias_part = wg[...], bg[...]
    for h in range(2):
        lanes = slice(h * LANES, (h + 1) * LANES)
        part[h, 0:GROUP] = weight_part[:, lanes].reshape(GROUP, 8, LANES)
        part[h, GROUP] = jnp.broadcast_to(bias_part[:, lanes], (8, LANES))
    store_hidden = pltpu.make_async_copy(hidden_v, hidden_out, local_sem.at[0])
    store_hidden.start()

    sent.append(send(part.at[1 - core], pair, pair_sem, 0, c_dev))
    arrived(pair, pair_sem, 0, c_dev)
    red[...] = part[core] + pair[...]

    group, member = lax.div(row, 8), a * 8 + lax.rem(row, 8)

    def at(member_now, group_now):
        return (lax.div(member_now, 8) * 2 + core, group_now * 8 + lax.rem(member_now, 8))

    head = at(0, group)
    def loop(act):
        def body(i, carry):
            act(i)
            return carry

        lax.fori_loop(1, GROUP, body, 0)

    def scatter(i):
        peer = lax.rem(member + i, GROUP)
        return remote(red.at[peer], scattered.at[member], rs_sem, i, at(peer, group))

    loop(lambda i: scatter(i).start())

    @pl.when(member != 0)
    def _():
        copy = pltpu.make_async_remote_copy(
            src_ref=red.at[GROUP],
            dst_ref=bias_in.at[member],
            send_sem=rb_sem.at[0, 0],
            recv_sem=rb_sem.at[1, member],
            device_id=head,
            device_id_type=MESH,
        )
        copy.start()
        copy.wait_send()

    scattered[member] = red[member]
    owned[1] = jnp.zeros((8, LANES), jnp.float32)
    def from_peer(ref, sems, i):
        peer = lax.rem(member + GROUP - i, GROUP)
        arrived(ref.at[peer], sems, i, at(peer, group))

    loop(lambda i: from_peer(scattered, rs_sem, i))
    owned[0] = jnp.sum(scattered[...], axis=0)

    @pl.when(member == 0)
    def _():
        bias_in[0] = red[GROUP]
        loop(lambda i: remote(bias_in.at[i], bias_in.at[i], rb_sem, i, c_dev).wait_recv())
        owned[1] = jnp.sum(bias_in[...], axis=0)

    n_group = n_row // 8
    if n_group > 1:
        for g in range(1, n_group):
            dev = at(member, lax.rem(group + g, n_group))
            sent.append(send(owned, crossed.at[g], cross_sem, g, dev))
        crossed[0] = owned[...]
        for g in range(1, n_group):
            arrived(crossed.at[g], cross_sem, g, at(member, lax.rem(group + n_group - g, n_group)))
        for g in range(1, n_group):
            sent.pop().wait_send()
        ordered = jnp.zeros(owned.shape, jnp.float32)
        for g in range(n_group):
            ordered = ordered + crossed[lax.rem(group + n_group - g, n_group)]
        owned[...] = ordered

    def spread(i):
        peer = lax.rem(member + i, GROUP)
        return remote(owned.at[0], fin.at[member], ag_sem, i, at(peer, group))

    loop(lambda i: spread(i).start())

    @pl.when(member == 0)
    def _():
        def spread_bias(i):
            return remote(owned.at[1], fin.at[GROUP], ab_sem, i, at(i, group))

        loop(lambda i: spread_bias(i).start())
        fin[GROUP] = owned[1]
        loop(lambda i: spread_bias(i).wait_send())

    @pl.when(member != 0)
    def _():
        pltpu.make_async_remote_copy(
            src_ref=owned.at[1],
            dst_ref=fin.at[GROUP],
            send_sem=ab_sem.at[0, 0],
            recv_sem=ab_sem.at[1, member],
            device_id=head,
            device_id_type=MESH,
        ).wait_recv()

    fin[member] = owned[0]
    loop(lambda i: from_peer(fin, ag_sem, i))
    sent.append(send(fin, fin_other, pair_sem, 1, c_dev))
    arrived(fin_other, pair_sem, 1, c_dev)
    mine, other = fin[...], fin_other[...]
    for h in range(2):
        half = jnp.where(core == h, mine, other)
        lanes = slice(h * LANES, (h + 1) * LANES)
        weight_out[:, lanes] = half[0:GROUP].reshape(GROUP * 8, LANES)
        bias_out[:, lanes] = half[GROUP, 0:1]
    for copy in sent:
        copy.wait_send()
    loop(lambda i: scatter(i).wait_send())
    loop(lambda i: spread(i).wait_send())
    all_sent()
    store_hidden.wait()


def hand_over(*refs):
    ins, outs, held, load_sem, store_sem = refs[0:3], refs[3:6], refs[6:9], refs[9], refs[10]
    loads = [pltpu.make_async_copy(ins[i], held[i], load_sem.at[i]) for i in range(3)]
    stores = [pltpu.make_async_copy(held[i], outs[i], store_sem.at[i]) for i in range(3)]
    for copy in loads:
        copy.start()
    for load, store in zip(loads, stores):
        load.wait()
        store.start()
    for copy in stores:
        copy.wait()


def local(n_row, features, tile_values, tile_row, tile_col, tile_count, weight, bias, cotangent):
    n_panel, slots, blk, _ = tile_values.shape
    rows, width = features.shape
    wide = weight.shape[1]
    n_z = n_row // 2
    n_group = n_row // 8
    dma = pltpu.SemaphoreType.DMA
    anywhere = pl.BlockSpec(memory_space=pl.ANY)
    smem = pl.BlockSpec(memory_space=pltpu.SMEM)
    vmem = pl.BlockSpec(memory_space=pltpu.VMEM)
    hidden, weight_grad, bias_grad = pl.pallas_call(
        functools.partial(kernel, n_row),
        out_shape=[
            jax.ShapeDtypeStruct((rows, wide), jnp.bfloat16),
            jax.ShapeDtypeStruct((width, wide), jnp.float32),
            jax.ShapeDtypeStruct((1, wide), jnp.float32),
        ],
        in_specs=[anywhere, anywhere, smem, smem, smem, anywhere, anywhere, anywhere],
        out_specs=[anywhere, vmem, vmem],
        scratch_shapes=[
            pltpu.VMEM((2 * n_row + 1, blk, width), jnp.bfloat16),
            pltpu.VMEM((2 * n_row + 1, blk, width), jnp.bfloat16),
            pltpu.VMEM((2 * n_row + 1, blk, width), jnp.bfloat16),
            pltpu.VMEM((2 * n_row + 1, blk, width), jnp.bfloat16),
            pltpu.VMEM((n_panel, slots, blk, blk), jnp.bfloat16),
            pltpu.VMEM((width, wide), jnp.bfloat16),
            pltpu.VMEM((1, wide), jnp.float32),
            pltpu.VMEM((rows, wide), jnp.bfloat16),
            pltpu.VMEM((rows, wide), jnp.bfloat16),
            pltpu.VMEM((blk, 2 * width), jnp.float32),
            pltpu.VMEM((2, GROUP + 1, 8, LANES), jnp.float32),
            pltpu.VMEM((GROUP + 1, 8, LANES), jnp.float32),
            pltpu.VMEM((GROUP + 1, 8, LANES), jnp.float32),
            pltpu.VMEM((GROUP, 8, LANES), jnp.float32),
            pltpu.VMEM((GROUP, 8, LANES), jnp.float32),
            pltpu.VMEM((2, 8, LANES), jnp.float32),
            pltpu.VMEM((n_group, 2, 8, LANES), jnp.float32),
            pltpu.VMEM((GROUP + 1, 8, LANES), jnp.float32),
            pltpu.VMEM((GROUP + 1, 8, LANES), jnp.float32),
            pltpu.VMEM((width, wide), jnp.float32),
            pltpu.VMEM((1, wide), jnp.float32),
            dma((4,)),
            dma((4,)),
            dma((2, 4 * n_z)),
            dma((2, 2 * n_z)),
            dma((2, 2 * n_z)),
            dma((2, n_z)),
            dma((2, n_z)),
            dma((2, 1)),
            dma((2, 4 * n_z)),
            dma((2, 2)),
            dma((2, GROUP)),
            dma((2, GROUP)),
            dma((2, n_group)),
            dma((2, GROUP)),
            dma((2, GROUP)),
        ],
        compiler_params=pltpu.CompilerParams(
            collective_id=0, has_side_effects=True, vmem_limit_bytes=56 * 1024 * 1024
        ),
    )(
        features.reshape(rows // blk, blk, width),
        tile_values,
        tile_row,
        tile_col,
        tile_count,
        weight,
        bias.reshape(1, wide),
        cotangent,
    )
    shapes = [jax.ShapeDtypeStruct(x.shape, x.dtype) for x in (hidden, weight_grad, bias_grad)]
    hidden, weight_grad, bias_grad = pl.pallas_call(
        hand_over,
        out_shape=shapes,
        in_specs=[anywhere] * 3,
        out_specs=[anywhere] * 3,
        scratch_shapes=[pltpu.VMEM(x.shape, x.dtype) for x in shapes] + [dma((3,)), dma((3,))],
        compiler_params=pltpu.CompilerParams(vmem_limit_bytes=60 * 1024 * 1024),
    )(hidden, weight_grad, bias_grad)
    return (hidden, weight_grad, bias_grad.reshape(wide))


def solution(mesh):
    in_specs = (
        P(("team", "row"), None),
        P(("team", "row"), None, None, None),
        P(("team", "row"), None),
        P(("team", "row"), None),
        P(("team", "row")),
        P(),
        P(),
        P(("team", "row"), None),
    )
    out_specs = (P(("team", "row"), None), P(), P())
    return jax.shard_map(
        functools.partial(local, mesh.shape["row"]),
        mesh=mesh,
        in_specs=in_specs,
        out_specs=out_specs,
        check_vma=False,
    )
```
